256 devices in a mesh: queue: 16 (over y_hi, x, core), space: 16 (over y_lo, z).
Axes of the slice: x: 4, y: 4 (y_hi: 2, y_lo: 2; y = y_hi * 2 + y_lo), z: 8, core: 2. Of those that a mesh axis runs over, the one named last changes fastest.
Arguments:
- latents: float32 [16, 4, 16, 48, 16], P('queue', None, None, 'space'), as said below
- fresh_noise: float32 [4, 16, 48, 16], P(None, None, 'space'), may hold values from -6 to 6
- timesteps: int32 [16], replicated, may hold values from 50 to 999, as said below
- queue_map: int32 [16], replicated, may hold values from 0 to 15, as said below
- conv_in_w: bfloat16 [3, 3, 4, 320], replicated, may hold values from -1 to 1
- time_w1: bfloat16 [320, 1280], replicated, may hold values from -0.3125 to 0.3125
- time_w2: bfloat16 [1280, 1280], replicated, may hold values from -0.15625 to 0.15625
- emb_w: bfloat16 [1280, 320], replicated, may hold values from -0.15625 to 0.15625
- conv1_w: bfloat16 [3, 3, 320, 320], replicated, may hold values from -0.109375 to 0.109375
- conv2_w: bfloat16 [3, 3, 320, 320], replicated, may hold values from -0.109375 to 0.109375
- qkv_w: bfloat16 [320, 960], replicated
- proj_w: bfloat16 [320, 320], replicated, may hold values from -0.3125 to 0.3125
- conv_out_w: bfloat16 [3, 3, 320, 4], replicated, may hold values from -0.109375 to 0.109375
Outputs:
- noise_pred: float32 [16, 4, 16, 48, 16], P('queue', None, None, 'space')
- next_queue: float32 [16, 4, 16, 48, 16], P('queue', None, None, 'space')
The draws below stay inside these ranges and needn't reach their ends.
Inputs may be any that keep to these rules, and one draw needn't show every extreme that they name: `queue_map`: each queue position names a different frame group. timesteps[queue_map[p]] rises strictly with the queue position p. Noisy latents.
All inputs are finite; a program needn't handle non-finite values.
Results may differ from the reference program's by a relative error of at most 0.0095.
Values may be sent and summed in bfloat16 or wider, within the bound.
A program may use at most 64 MiB of HBM per device.

```python
import math
import jax
import jax.numpy as jnp
from jax import lax

CH = 320
GROUPS = 32
HEAD_DIM = 64
FRAMES = 16
ROWS_DEV = 3
COLS = 16
STEP = 50
TEMB = 1280
QUEUE = 16
ROWS = 48


def queue_levels(key):
    order_map = jax.random.permutation(jax.random.fold_in(key, 11), QUEUE).astype(jnp.int32)
    spacing = (1000 - STEP) // QUEUE
    slots = jnp.arange(QUEUE, dtype=jnp.int32)
    offsets = jax.random.randint(jax.random.fold_in(key, 12), (QUEUE,), 0, spacing, dtype=jnp.int32)
    levels = STEP + slots * spacing + offsets
    levels = jnp.where(slots == 0, STEP, levels)
    levels = jnp.where(slots == QUEUE - 1, 999, levels)
    by_group = jnp.zeros((QUEUE,), jnp.int32).at[order_map].set(levels)
    return (order_map, by_group)


def draw_queue_map(key, part):
    order_map, by_group = queue_levels(key)
    return order_map


def draw_timesteps(key, part):
    order_map, by_group = queue_levels(key)
    return by_group


def draw_latents(key, part):
    key = jax.random.fold_in(key, 3)
    shape = (QUEUE, 4, FRAMES, ROWS, COLS)
    block_count = ROWS // ROWS_DEV
    block_gain = jnp.exp(jax.random.uniform(jax.random.fold_in(key, 5), (QUEUE, block_count), jnp.float32, -1.5, 1.5))
    row_gain = jnp.repeat(block_gain, ROWS_DEV, axis=1)[:, None, None, :, None]
    values = jax.random.normal(key, shape, jnp.float32) * row_gain
    return values.astype(jnp.float32)


def draw_qkv_w(key, part):
    key = jax.random.fold_in(key, 7)
    subkeys = jax.random.split(key, 3)
    query_w = jax.random.normal(subkeys[0], (CH, CH), jnp.float32) * CH ** (-0.5)
    key_w = jax.random.normal(subkeys[1], (CH, CH), jnp.float32) * CH ** (-0.5)
    value_w = jax.random.normal(subkeys[2], (CH, CH), jnp.float32) * CH ** (-0.5)
    return jnp.concatenate([query_w, key_w, value_w], axis=1).astype(jnp.bfloat16)


def steps_of(own_key, dims, cuts, low, largest):
    gain = 1.0
    for dim, shards_of in cuts:
        heights = jax.random.uniform(jax.random.fold_in(jax.random.fold_in(own_key, 6), dim), (shards_of,), jnp.float32, low / len(cuts), largest / len(cuts))
        gain = gain * jnp.repeat(jnp.exp(heights), dims[dim] // shards_of).reshape((-1,) + (1,) * (len(dims) - 1 - dim))
    return gain


def normal_values(rng, shape, scale, limit, cuts=(), kind=jnp.bfloat16):
    level = steps_of(rng, shape, cuts, -0.22, 0.18) if cuts else 1.0
    values = jax.random.normal(rng, shape, jnp.float32) * scale * level
    return jnp.minimum(jnp.maximum(values, -limit), limit).astype(kind)


def setup_inputs(seed: int = 0) -> dict:
    key_of = jax.random.split(jax.random.key(seed), 14)
    return {
        "latents": draw_latents(jax.random.fold_in(key_of[13], 71), 0),
        "fresh_noise": normal_values(key_of[1], (4, FRAMES, ROWS, COLS), 1.0, 6.0, ((2, 16),), jnp.float32),
        "timesteps": draw_timesteps(jax.random.fold_in(key_of[13], 71), 0),
        "queue_map": draw_queue_map(jax.random.fold_in(key_of[13], 71), 0),
        "conv_in_w": normal_values(key_of[4], (3, 3, 4, CH), 36 ** -0.5, 1.0),
        "time_w1": normal_values(key_of[5], (CH, TEMB), CH ** -0.5, 0.3125),
        "time_w2": normal_values(key_of[6], (TEMB, TEMB), TEMB ** -0.5, 0.15625),
        "emb_w": normal_values(key_of[7], (TEMB, CH), TEMB ** -0.5, 0.15625),
        "conv1_w": normal_values(key_of[8], (3, 3, CH, CH), (9 * CH) ** -0.5, 0.109375),
        "conv2_w": normal_values(key_of[9], (3, 3, CH, CH), (9 * CH) ** -0.5, 0.109375),
        "qkv_w": draw_qkv_w(jax.random.fold_in(key_of[13], 71), 0),
        "proj_w": normal_values(key_of[11], (CH, CH), CH ** -0.5, 0.3125),
        "conv_out_w": normal_values(key_of[12], (3, 3, CH, 4), (9 * CH) ** -0.5, 0.109375),
    }


NORM_EPS = 1e-05

def alpha_table():
    betas = jnp.linspace(0.00085 ** 0.5, 0.012 ** 0.5, 1000, dtype=jnp.float32) ** 2
    return jnp.cumprod(1.0 - betas)

def group_norm(features):
    shaped = features.reshape(features.shape[:3] + (GROUPS, features.shape[3] // GROUPS))
    centre = lax.optimization_barrier(jnp.mean(shaped, axis=(0, 1, 2, 4), keepdims=True))
    spread = lax.optimization_barrier(jnp.mean((shaped - centre) ** 2, axis=(0, 1, 2, 4), keepdims=True))
    return ((shaped - centre) * lax.rsqrt(spread + NORM_EPS)).reshape(features.shape)

def convolve(features, weight):
    padded = jnp.pad(features, ((0, 0), (1, 1), (1, 1), (0, 0)))
    frame_count, row_count, col_count, in_ch = features.shape
    accum = jnp.zeros((frame_count * row_count * col_count, weight.shape[3]), jnp.float32)
    for row_tap in range(3):
        for col_tap in range(3):
            window = padded[:, row_tap:row_tap + row_count, col_tap:col_tap + col_count, :]
            accum = accum + jnp.dot(window.reshape(-1, in_ch), weight[row_tap, col_tap], preferred_element_type=jnp.float32)
    return accum.reshape(frame_count, row_count, col_count, weight.shape[3])

def time_embedding(noise_level, time_w1, time_w2, emb_w):
    half_width = CH // 2
    frequency = jnp.exp(-math.log(10000.0) * jnp.arange(half_width, dtype=jnp.float32) / half_width)
    phases = noise_level.astype(jnp.float32) * frequency
    sinusoid = jnp.concatenate([jnp.cos(phases), jnp.sin(phases)])[None].astype(jnp.bfloat16)
    first_hidden = jax.nn.silu(jnp.dot(sinusoid, time_w1, preferred_element_type=jnp.float32)).astype(jnp.bfloat16)
    second = jax.nn.silu(jnp.dot(first_hidden, time_w2, preferred_element_type=jnp.float32)).astype(jnp.bfloat16)
    return jnp.dot(second, emb_w, preferred_element_type=jnp.float32)[0]

def attend(attn_in, qkv_w, proj_w):
    frame_count, row_count, col_count, channels = attn_in.shape
    projected = jnp.dot(attn_in.reshape(-1, channels), qkv_w, preferred_element_type=jnp.float32).astype(jnp.bfloat16)
    projected = projected.reshape(frame_count, row_count, col_count, 3, channels // HEAD_DIM, HEAD_DIM)
    queries = projected[:, :, :, 0].astype(jnp.float32)
    keys_all = projected[:, :, :, 1].astype(jnp.float32)
    values = projected[:, :, :, 2].astype(jnp.float32)
    scores = jnp.einsum('fhwnd,ghwnd->hwnfg', queries, keys_all) * HEAD_DIM ** (-0.5)
    probs = jax.nn.softmax(scores, axis=-1).astype(jnp.bfloat16)
    probs = lax.optimization_barrier(probs).astype(jnp.float32)
    attended = jnp.einsum('hwnfg,ghwnd->fhwnd', probs, values).astype(jnp.bfloat16)
    attended = attended.reshape(-1, channels)
    return jnp.dot(attended, proj_w, preferred_element_type=jnp.float32).reshape(attn_in.shape)

def predict(latent, noise_level, conv_in_w, time_w1, time_w2, emb_w, conv1_w, conv2_w, qkv_w, proj_w, conv_out_w):
    latent_in = jnp.transpose(latent.astype(jnp.bfloat16), (1, 2, 3, 0))
    stream = convolve(latent_in, conv_in_w)
    time_bias = time_embedding(noise_level, time_w1, time_w2, emb_w)
    normed1 = jax.nn.silu(group_norm(stream)).astype(jnp.bfloat16)
    hidden1 = convolve(normed1, conv1_w) + time_bias
    normed2 = jax.nn.silu(group_norm(hidden1)).astype(jnp.bfloat16)
    block_out = stream + convolve(normed2, conv2_w)
    mixed = block_out + attend(group_norm(block_out).astype(jnp.bfloat16), qkv_w, proj_w)
    normed3 = jax.nn.silu(group_norm(mixed)).astype(jnp.bfloat16)
    return jnp.transpose(convolve(normed3, conv_out_w), (3, 0, 1, 2))

def reference(latents, fresh_noise, timesteps, queue_map, conv_in_w, time_w1, time_w2, emb_w, conv1_w, conv2_w, qkv_w, proj_w, conv_out_w):
    alphas = alpha_table()

    def advance(position):
        noise_level = timesteps[queue_map[position]]
        latent = latents[position]
        noise_pred = predict(latent, noise_level, conv_in_w, time_w1, time_w2, emb_w, conv1_w, conv2_w, qkv_w, proj_w, conv_out_w)
        alpha_now = alphas[noise_level]
        alpha_next = alphas[noise_level - STEP]
        advanced = jnp.sqrt(alpha_next / alpha_now) * (latent - jnp.sqrt(1.0 - alpha_now) * noise_pred) + jnp.sqrt(1.0 - alpha_next) * noise_pred
        return (noise_pred, advanced)
    noise_all, advanced_all = lax.map(advance, jnp.arange(QUEUE, dtype=jnp.int32))
    next_queue = jnp.concatenate([fresh_noise[None], advanced_all[:-1]], axis=0)
    return (noise_all, next_queue)
```

```python
import functools
import math

import jax
import jax.numpy as jnp
from jax import lax
from jax.experimental import pallas as pl
from jax.experimental.pallas import tpu as pltpu
from jax.sharding import PartitionSpec as P

GROUPS = 32
HEAD_DIM = 64
STEP = 50
NORM_EPS = 1e-05
MESH = pl.DeviceIdType.MESH

CH = 320
FRAMES = 16
COLS = 16
ROWS = 3
CELLS = FRAMES * COLS
PER_GROUP = CH // GROUPS
HEADS = CH // HEAD_DIM
MAIN = 256
REST = CH - MAIN
BF = jnp.bfloat16
F32 = jnp.float32


def dot(a, b):
    return jnp.dot(a, b, preferred_element_type=F32)


def dot_nt(a, b):
    return lax.dot_general(a, b, (((1,), (1,)), ((), ())), preferred_element_type=F32)


def silu_of_half(h):
    return h + h * jnp.tanh(h)


def iota(shape, dim):
    return lax.broadcasted_iota(jnp.int32, shape, dim)


def split3(v):
    hi = v.astype(BF)
    left = v - hi.astype(F32)
    mid = left.astype(BF)
    return hi, mid, (left - mid.astype(F32)).astype(BF)


def kernel(
    nq,
    ns,
    ts_ref,
    map_ref,
    lat_hbm,
    cin_hbm,
    tw1_hbm,
    tw2_hbm,
    emb_hbm,
    c1_hbm,
    c2_hbm,
    qkv_hbm,
    proj_hbm,
    cout_hbm,
    noise_ref,
    next_ref,
    lat_v,
    cin_v,
    tw1_v,
    tw2_v,
    emb_v,
    c1_v,
    c2_v,
    qkv_v,
    proj_v,
    cout_v,
    load_sem,
    lat_f,
    lat_b,
    xt,
    cin_f,
    cin_w,
    stream,
    hidden,
    block,
    xm,
    xr,
    kr,
    nr,
    wk,
    pairs,
    bias,
    cout_f,
    wout,
    attended,
    rows_st,
    stats,
    edge_raw,
    edge_scaled,
    edge_in,
    edge_next,
    main_out,
    main_in,
    lat_send,
    lat_recv,
    stat_send,
    stat_recv,
    edge_send,
    edge_recv,
    main_send,
    main_recv,
):
    q = lax.axis_index("queue")
    s = lax.axis_index("space")
    up = lax.rem(s + ns - 1, ns)
    down = lax.rem(s + 1, ns)
    ahead = lax.rem(q + 1, nq)
    behind = lax.rem(q + nq - 1, nq)
    first = s == 0
    last = s == ns - 1

    barrier = pltpu.get_barrier_semaphore()

    def greet(j, _):
        peer = lax.rem(s + j, ns)
        pl.semaphore_signal(barrier, inc=1, device_id=(q, peer), device_id_type=MESH)
        return 0

    lax.fori_loop(1, ns, greet, 0)
    for peer in (up, s, down):
        pl.semaphore_signal(barrier, inc=1, device_id=(behind, peer), device_id_type=MESH)

    loads = [
        pltpu.make_async_copy(src, dst, load_sem.at[i])
        for i, (src, dst) in enumerate(
            (
                (lat_hbm, lat_v),
                (cin_hbm, cin_v),
                (tw1_hbm, tw1_v),
                (tw2_hbm, tw2_v),
                (emb_hbm, emb_v),
                (c1_hbm, c1_v),
                (c2_hbm, c2_v),
                (qkv_hbm, qkv_v),
                (proj_hbm, proj_v),
                (cout_hbm, cout_v),
            )
        )
    ]
    for load in loads:
        load.start()
    load_lat, load_cin, load_tw1, load_tw2, load_emb, load_c1, load_c2, load_qkv, load_proj, load_cout = loads

    load_lat.wait()
    lat_f[12:16, :] = jnp.zeros((4, CELLS), F32)
    for f in range(FRAMES):
        lat_f[0:12, f * COLS : (f + 1) * COLS] = lat_v[pl.ds(f, 12, stride=FRAMES), :]
    lat_b[1] = lat_f[...].astype(BF)

    pl.semaphore_wait(barrier, ns - 1 + 3)

    lat_down = pltpu.make_async_remote_copy(
        lat_b.at[1], lat_b.at[0], lat_send.at[0], lat_recv.at[0], device_id=(q, down), device_id_type=MESH
    )
    lat_up = pltpu.make_async_remote_copy(
        lat_b.at[1], lat_b.at[2], lat_send.at[1], lat_recv.at[1], device_id=(q, up), device_id_type=MESH
    )
    lat_down.start()
    lat_up.start()

    ci = iota((CH, CH), 0) * 6554 >> 16
    cj = iota((CH, CH), 1) * 6554 >> 16
    pairs[...] = jnp.where(ci == cj, 1.0, 0.0).astype(BF)

    load_cin.wait()
    cin_f[36:40, :] = jnp.zeros((4, CH), F32)
    for a in range(3):
        for b in range(3):
            t = a * 3 + b
            cin_f[t * 4 : t * 4 + 4, :] = cin_v[a, b].astype(F32)

    kk = iota((128, 40), 0)
    jj = iota((128, 40), 1)
    tap_b = jnp.where(kk >= 36, 1, 0) + jnp.where(kk >= 72, 1, 0)
    left = kk - 36 * tap_b
    part = left * 5462 >> 16
    left = left - 12 * part
    chan = left * 21846 >> 16
    row_of = 3 * part + left - 3 * chan

    def place_cin(y, _):
        tap_a = row_of - y
        hit = (tap_a >= 0) & (tap_a < 3) & (jj == (tap_a * 3 + tap_b) * 4 + chan)
        sel = jnp.where(hit, 1.0, 0.0).astype(BF)
        cin_w[y] = dot(sel, cin_f[...].astype(BF)).astype(BF)
        return 0

    lax.fori_loop(0, 7, place_cin, 0)

    xr[:, :, 192:256] = jnp.zeros((9, CELLS, 64), BF)

    def shared_passes(which, w):
        for b in range(3):
            for a in range(3):
                kr[which, b, a * REST : (a + 1) * REST, :] = w[a, b, MAIN:CH, 0:MAIN]
            kr[which, b, 3 * REST : 256, :] = jnp.zeros((256 - 3 * REST, MAIN), BF)
        for a in range(3):
            for b in range(3):
                nr[which, a * 256 : (a + 1) * 256, b * REST : (b + 1) * REST] = w[a, b, 0:MAIN, MAIN:CH]
                nr[which, 768 + a * REST : 768 + (a + 1) * REST, b * REST : (b + 1) * REST] = w[
                    a, b, MAIN:CH, MAIN:CH
                ]
        nr[which, :, 3 * REST : 256] = jnp.zeros((1024, 256 - 3 * REST), BF)
        nr[which, 768 + 3 * REST : 1024, :] = jnp.zeros((256 - 3 * REST, 256), BF)

    lat_down.wait_recv()
    lat_up.wait_recv()
    lane = iota((16, CELLS), 1) & (COLS - 1)
    xt[108:128, :] = jnp.zeros((20, CELLS), F32)
    for n in range(3):
        v = lat_b[n].astype(F32)
        if n == 0:
            v = jnp.where(first, 0.0, v)
        if n == 2:
            v = jnp.where(last, 0.0, v)
        shifted = (
            jnp.where(lane == 0, 0.0, pltpu.roll(v, 1, 1)),
            v,
            jnp.where(lane == COLS - 1, 0.0, pltpu.roll(v, CELLS - 1, 1)),
        )
        for b in range(3):
            xt[b * 36 + n * 12 : b * 36 + n * 12 + 12, :] = shifted[b][0:12]
    x_in = xt[...].T.astype(BF)

    def row_stats(r, x):
        m = jnp.sum(x, axis=0, keepdims=True) * (1.0 / CELLS)
        rows_st[0, pl.ds(r, 1), :] = m
        rows_st[1, pl.ds(r, 1), :] = jnp.sum((x - m) ** 2, axis=0, keepdims=True)

    def send_stats(phase):
        m = rows_st[0, 0:ROWS, :]
        mean = jnp.sum(m, axis=0, keepdims=True) * (1.0 / ROWS)
        dev = jnp.sum(rows_st[1, 0:ROWS, :] + CELLS * (m - mean) ** 2, axis=0, keepdims=True)
        stats[phase, s] = jnp.concatenate([mean, dev], axis=0)

        def send(j, _):
            peer = lax.rem(s + j, ns)
            pltpu.make_async_remote_copy(
                stats.at[phase, s],
                stats.at[phase, s],
                stat_send.at[phase],
                stat_recv.at[phase],
                device_id=(q, peer),
                device_id_type=MESH,
            ).start()
            return 0

        lax.fori_loop(1, ns, send, 0)
        near = dot(jnp.broadcast_to(mean, (16, CH)).astype(BF), pairs[...])
        return near[0:1] * (1.0 / PER_GROUP)

    def take_stats(phase, near):
        pltpu.make_async_copy(
            stats.at[phase, pl.ds(0, ns - 1)], stats.at[phase, pl.ds(0, ns - 1)], stat_recv.at[phase]
        ).wait()
        v = stats[phase]
        d = v[:, 0, :] - near
        s1 = jnp.sum(d, axis=0, keepdims=True)
        s2 = jnp.sum(v[:, 1, :] + (ROWS * CELLS) * (d * d), axis=0, keepdims=True)
        parts = split3(s1) + split3(s2)
        stacked = jnp.concatenate([p.astype(F32) for p in parts] + [jnp.zeros((10, CH), F32)], axis=0)
        g = dot(stacked.astype(BF), pairs[...])
        off = (g[0:1] + g[1:2] + g[2:3]) * (1.0 / (ns * PER_GROUP))
        spread = (g[3:4] + g[4:5] + g[5:6]) * (1.0 / (ns * PER_GROUP * ROWS * CELLS)) - off * off
        return near + off, lax.rsqrt(jnp.maximum(spread, 0.0) + NORM_EPS)

    def stats_sent(phase):
        pltpu.make_async_copy(
            stats.at[phase, pl.ds(0, ns - 1)], stats.at[phase, pl.ds(0, ns - 1)], stat_send.at[phase]
        ).wait()

    def put_normed(r, y):
        yb = y.astype(BF)
        xm[r] = yb[:, 0:MAIN]
        rest = yb[:, MAIN:CH]
        xr[r + 2, :, 0:REST] = rest
        xr[r + 1, :, REST : 2 * REST] = rest
        xr[r, :, 2 * REST : 3 * REST] = rest

    def column(width, x):
        return jnp.where((iota((CELLS, width), 0) & (COLS - 1)) == x, 0.0, 1.0)

    def conv_row(which, w, y):
        x = jnp.concatenate([xm[y], xm[y + 1], xm[y + 2], xr[y + 2]], axis=1)
        z = [
            dot(
                x,
                jnp.concatenate(
                    [w[0, b, 0:MAIN, 0:MAIN], w[1, b, 0:MAIN, 0:MAIN], w[2, b, 0:MAIN, 0:MAIN], kr[which, b]], axis=0
                ),
            )
            for b in range(3)
        ]
        main = z[1] + column(MAIN, 0) * pltpu.roll(z[0], 1, 0) + column(MAIN, COLS - 1) * pltpu.roll(z[2], CELLS - 1, 0)
        zr = dot(x, nr[which])
        rest = (
            column(REST, 0) * pltpu.roll(zr, 1, 0)[:, 0:REST]
            + zr[:, REST : 2 * REST]
            + column(REST, COLS - 1) * pltpu.roll(zr, CELLS - 1, 0)[:, 2 * REST : 3 * REST]
        )
        return main, rest

    def stream_row(y):
        v = dot(x_in, cin_w[y])
        stream[y] = v
        return v

    def own_stream(i, _):
        row_stats(i, stream_row(i + 2))
        return 0

    lax.fori_loop(0, ROWS, own_stream, 0)
    near1 = send_stats(0)

    for y in (0, 1, 5, 6):
        stream_row(y)

    level = ts_ref[map_ref[q]]
    pos = iota((16, CH), 1)
    half = CH // 2
    k = jnp.where(pos < half, pos, pos - half).astype(F32)
    phases = level.astype(F32) * jnp.exp(k * (-math.log(10000.0) / half))
    sinusoid = jnp.where(pos < half, jnp.cos(phases), jnp.sin(phases)).astype(BF)
    load_tw1.wait()
    h = dot(sinusoid, tw1_v[...])
    first_hidden = silu_of_half(0.5 * h).astype(BF)
    load_tw2.wait()
    h = dot(first_hidden, tw2_v[...])
    second = silu_of_half(0.5 * h).astype(BF)
    load_emb.wait()
    bias[...] = dot_nt(second, emb_v[...])[0:1]
    load_c1.wait()
    shared_passes(0, c1_v)

    mean, inv = take_stats(0, near1)
    half_inv = 0.5 * inv

    def norm1(r, _):
        y = silu_of_half((stream[r] - mean) * half_inv)
        row = s * ROWS + r - 2
        put_normed(r, jnp.where((row >= 0) & (row < ns * ROWS), y, 0.0))
        return 0

    lax.fori_loop(0, 7, norm1, 0)

    def hidden_row(j):
        main, rest = conv_row(0, c1_v, j)
        hidden[j, :, 0:MAIN] = main + bias[:, 0:MAIN]
        hidden[j, :, MAIN:CH] = rest + bias[:, MAIN:CH]

    def own_hidden(i, _):
        hidden_row(i + 1)
        row_stats(i, hidden[i + 1])
        return 0

    lax.fori_loop(0, ROWS, own_hidden, 0)
    near2 = send_stats(1)

    def halo_hidden(i, _):
        hidden_row(i * 4)
        return 0

    lax.fori_loop(0, 2, halo_hidden, 0)
    load_c2.wait()
    shared_passes(1, c2_v)

    mean2, inv2 = take_stats(1, near2)
    half_inv2 = 0.5 * inv2

    def norm2(r, _):
        y = silu_of_half((hidden[r] - mean2) * half_inv2)
        row = s * ROWS + r - 1
        put_normed(r, jnp.where((row >= 0) & (row < ns * ROWS), y, 0.0))
        return 0

    lax.fori_loop(0, 5, norm2, 0)

    def block_row(i, _):
        main, rest = conv_row(1, c2_v, i)
        block[i, :, 0:MAIN] = stream[i + 2, :, 0:MAIN] + main
        block[i, :, MAIN:CH] = stream[i + 2, :, MAIN:CH] + rest
        row_stats(i, block[i])
        return 0

    lax.fori_loop(0, ROWS, block_row, 0)
    near3 = send_stats(2)

    load_qkv.wait()
    wk[...] = qkv_v[:, CH : 2 * CH]
    load_proj.wait()
    load_cout.wait()
    cout_f[36:40, :] = jnp.zeros((4, CH), F32)
    for a in range(3):
        for b in range(3):
            r = (a * 3 + b) * 4
            cout_f[r : r + 4, :] = cout_v[a, b].astype(F32)
    to = iota((144, 40), 0)
    src = iota((144, 40), 1)
    to_b = jnp.where(to >= 48, 1, 0) + jnp.where(to >= 96, 1, 0)
    to_part = to - 48 * to_b >> 4
    to_row = to & 15
    to_c = to_row * 21846 >> 16
    to_y = to_row - 3 * to_c + jnp.where(to_part == 1, ROWS, 0) - jnp.where(to_part == 2, ROWS, 0)
    for i in range(ROWS):
        tap = i - to_y + 1
        hit = (tap >= 0) & (tap < 3) & (to_row < 12) & (src == (tap * 3 + to_b) * 4 + to_c)
        wout[i] = dot(jnp.where(hit, 1.0, 0.0).astype(BF), cout_f[...].astype(BF)).astype(BF)

    step_of = iota((8, 128), 0) * 128 + iota((8, 128), 1)
    lo, hi = 0.00085**0.5, 0.012**0.5
    beta = (lo + step_of.astype(F32) * ((hi - lo) / 999.0)) ** 2

    def alpha(t):
        v = jnp.where(step_of <= t, 1.0 - beta, 1.0)
        for sh in (64, 32, 16, 8, 4, 2, 1):
            v = v * pltpu.roll(v, sh, 1)
        for sh in (4, 2, 1):
            v = v * pltpu.roll(v, sh, 0)
        return v[0:1, 0:1]

    alpha_now = alpha(level)
    alpha_next = alpha(level - STEP)
    keep = jnp.sqrt(alpha_next / alpha_now)
    gain = jnp.sqrt(1.0 - alpha_next) - keep * jnp.sqrt(1.0 - alpha_now)

    mean3, inv3 = take_stats(2, near3)

    same = ((iota((CELLS, CELLS), 0) ^ iota((CELLS, CELLS), 1)) & (COLS - 1)) == 0
    low_half = iota((CELLS, 128), 1) < HEAD_DIM

    def attend_row(i, _):
        x = ((block[i] - mean3) * inv3).astype(BF)
        query = (dot(x, qkv_v[:, 0:CH]) * HEAD_DIM**-0.5).astype(BF)
        key = dot(x, wk[...]).astype(BF)
        value = dot(x, qkv_v[:, 2 * CH : 3 * CH]).astype(BF)
        ones = jnp.ones((CELLS, 128), BF)
        for t in range(3):
            width = min(128, CH - t * 128)
            lanes = slice(t * 128, t * 128 + width)
            qt, kt, vt = query[:, lanes], key[:, lanes], value[:, lanes]
            if width < 128:
                vt = jnp.concatenate([vt, jnp.zeros((CELLS, 128 - width), BF)], axis=1)
            vt = jnp.concatenate([vt, ones], axis=1)
            outs = []
            for part in range(width // HEAD_DIM):
                qh = qt
                if width == 128:
                    qh = jnp.where(low_half if part == 0 else jnp.logical_not(low_half), qt, jnp.zeros_like(qt))
                sc = jnp.where(same, dot_nt(qh, kt), -1e30)
                p = jnp.exp(sc - jnp.max(sc, axis=1, keepdims=True)).astype(BF)
                o = dot(p, vt)
                outs.append(o[:, 0:128] / o[:, 128:256])
            o = outs[0] if len(outs) == 1 else jnp.where(low_half, outs[0], outs[1])
            attended[:, lanes] = o[:, 0:width].astype(BF)
        mixed = block[i] + dot(attended[...], proj_v[...])
        block[i] = mixed
        row_stats(i, mixed)
        return 0

    lax.fori_loop(0, ROWS, attend_row, 0)
    near4 = send_stats(3)
    mean4, inv4 = take_stats(3, near4)
    half_inv4 = 0.5 * inv4

    z = jnp.zeros((144, CELLS), F32)
    for i in range(ROWS):
        z = z + dot_nt(wout[i], silu_of_half((block[i] - mean4) * half_inv4).astype(BF))
    lane = iota((48, CELLS), 1) & (COLS - 1)
    sums = (
        z[48:96]
        + jnp.where(lane == 0, 0.0, pltpu.roll(z[0:48], 1, 1))
        + jnp.where(lane == COLS - 1, 0.0, pltpu.roll(z[96:144], CELLS - 1, 1))
    )
    own = sums[0:16]
    for side in range(2):
        edge_raw[side] = sums[16 + 16 * side : 32 + 16 * side]
        edge_scaled[side] = gain * sums[16 + 16 * side : 32 + 16 * side]
    sends = []
    for side, peer in ((0, down), (1, up)):
        sends.append(
            pltpu.make_async_remote_copy(
                edge_scaled.at[side],
                edge_next.at[side],
                edge_send.at[side],
                edge_recv.at[side],
                device_id=(ahead, peer),
                device_id_type=MESH,
            )
        )
        sends.append(
            pltpu.make_async_remote_copy(
                edge_raw.at[side],
                edge_in.at[side],
                edge_send.at[2 + side],
                edge_recv.at[2 + side],
                device_id=(q, peer),
                device_id_type=MESH,
            )
        )
    for send in sends:
        send.start()
    main_out[...] = keep * lat_f[...] + gain * own
    main_send_copy = pltpu.make_async_remote_copy(
        main_out, main_in, main_send, main_recv, device_id=(ahead, s), device_id_type=MESH
    )
    main_send_copy.start()

    def put(out, v):
        for f in range(FRAMES):
            out[pl.ds(f, 12, stride=FRAMES), :] = v[0:12, f * COLS : (f + 1) * COLS]

    sends[1].wait_recv()
    sends[3].wait_recv()
    put(noise_ref, own + jnp.where(first, 0.0, edge_in[0]) + jnp.where(last, 0.0, edge_in[1]))
    main_send_copy.wait_recv()
    sends[0].wait_recv()
    sends[2].wait_recv()
    put(next_ref, main_in[...] + jnp.where(first, 0.0, edge_next[0]) + jnp.where(last, 0.0, edge_next[1]))

    lat_down.wait_send()
    lat_up.wait_send()
    for phase in range(4):
        stats_sent(phase)
    for send in sends:
        send.wait_send()
    main_send_copy.wait_send()


def per_device(
    nq,
    ns,
    latents,
    fresh_noise,
    timesteps,
    queue_map,
    conv_in_w,
    time_w1,
    time_w2,
    emb_w,
    conv1_w,
    conv2_w,
    qkv_w,
    proj_w,
    conv_out_w,
):
    smem = pl.BlockSpec(memory_space=pltpu.SMEM)
    hbm = pl.BlockSpec(memory_space=pl.ANY)
    vmem = pl.BlockSpec(memory_space=pltpu.VMEM)
    latents = jnp.transpose(latents[0], (0, 2, 1, 3)).reshape(4 * ROWS * FRAMES, COLS)
    emb_t = emb_w.T
    out_t = jnp.swapaxes(conv_out_w, 2, 3)
    weights = (conv_in_w, time_w1, time_w2, emb_t, conv1_w, conv2_w, qkv_w, proj_w, out_t)
    DMA = pltpu.SemaphoreType.DMA
    noise, nxt = pl.pallas_call(
        functools.partial(kernel, nq, ns),
        out_shape=(
            jax.ShapeDtypeStruct((4 * ROWS * FRAMES, COLS), F32),
            jax.ShapeDtypeStruct((4 * ROWS * FRAMES, COLS), F32),
        ),
        in_specs=[smem, smem] + [hbm] * (1 + len(weights)),
        out_specs=(vmem, vmem),
        scratch_shapes=[pltpu.VMEM(latents.shape, F32)]
        + [pltpu.VMEM(w.shape, BF) for w in weights]
        + [
            DMA((1 + len(weights),)),
            pltpu.VMEM((16, CELLS), F32),
            pltpu.VMEM((3, 16, CELLS), BF),
            pltpu.VMEM((128, CELLS), F32),
            pltpu.VMEM((40, CH), F32),
            pltpu.VMEM((7, 128, CH), BF),
            pltpu.VMEM((7, CELLS, CH), F32),
            pltpu.VMEM((5, CELLS, CH), F32),
            pltpu.VMEM((3, CELLS, CH), F32),
            pltpu.VMEM((7, CELLS, MAIN), BF),
            pltpu.VMEM((9, CELLS, 256), BF),
            pltpu.VMEM((2, 3, 256, MAIN), BF),
            pltpu.VMEM((2, 1024, 256), BF),
            pltpu.VMEM((CH, CH), BF),
            pltpu.VMEM((CH, CH), BF),
            pltpu.VMEM((1, CH), F32),
            pltpu.VMEM((40, CH), F32),
            pltpu.VMEM((3, 144, CH), BF),
            pltpu.VMEM((CELLS, CH), BF),
            pltpu.VMEM((2, 8, CH), F32),
            pltpu.VMEM((4, ns, 2, CH), F32),
            pltpu.VMEM((2, 16, CELLS), F32),
            pltpu.VMEM((2, 16, CELLS), F32),
            pltpu.VMEM((2, 16, CELLS), F32),
            pltpu.VMEM((2, 16, CELLS), F32),
            pltpu.VMEM((16, CELLS), F32),
            pltpu.VMEM((16, CELLS), F32),
            DMA((2,)),
            DMA((2,)),
            DMA((4,)),
            DMA((4,)),
            DMA((4,)),
            DMA((4,)),
            DMA,
            DMA,
        ],
        compiler_params=pltpu.CompilerParams(
            collective_id=0, has_side_effects=True, vmem_limit_bytes=60 * 1024 * 1024
        ),
        cost_estimate=pl.CostEstimate(flops=10**10, bytes_accessed=10**7, transcendentals=10**6),
    )(timesteps, queue_map, latents, *weights)

    def as_frames(v):
        return jnp.transpose(v.reshape(4, ROWS, FRAMES, COLS), (0, 2, 1, 3))

    next_queue = jnp.where(lax.axis_index("queue") == 0, fresh_noise, as_frames(nxt))
    return as_frames(noise)[None], next_queue[None]


def solution(mesh):
    nq, ns = mesh.shape["queue"], mesh.shape["space"]
    rows = P("queue", None, None, "space", None)
    return jax.shard_map(
        functools.partial(per_device, nq, ns),
        mesh=mesh,
        in_specs=(rows, P(None, None, "space", None)) + (P(),) * 11,
        out_specs=(rows, rows),
        check_vma=False,
    )
```

```python
import functools
import math

import jax
import jax.numpy as jnp
from jax import lax
from jax.experimental import pallas as pl
from jax.experimental.pallas import tpu as pltpu
from jax.sharding import PartitionSpec as P

GROUPS = 32
HEAD_DIM = 64
STEP = 50
NORM_EPS = 1e-05
MESH = pl.DeviceIdType.MESH

CH = 320
FRAMES = 16
COLS = 16
ROWS = 3
CELLS = FRAMES * COLS
PER_GROUP = CH // GROUPS
HEADS = CH // HEAD_DIM
MAIN = 256
REST = CH - MAIN
BF = jnp.bfloat16
F32 = jnp.float32


def dot(a, b):
    return jnp.dot(a, b, preferred_element_type=F32)


def dot_nt(a, b):
    return lax.dot_general(a, b, (((1,), (1,)), ((), ())), preferred_element_type=F32)


def silu_of_half(h):
    return h + h * jnp.tanh(h)


def iota(shape, dim):
    return lax.broadcasted_iota(jnp.int32, shape, dim)


def split3(v):
    hi = v.astype(BF)
    left = v - hi.astype(F32)
    mid = left.astype(BF)
    return hi, mid, (left - mid.astype(F32)).astype(BF)


def kernel(
    nq,
    ns,
    ts_hbm,
    map_hbm,
    lat_hbm,
    cin_hbm,
    tw1_hbm,
    tw2_hbm,
    emb_hbm,
    c1_hbm,
    c2_hbm,
    qkv_hbm,
    proj_hbm,
    cout_hbm,
    noise_ref,
    next_ref,
    ts_ref,
    map_ref,
    lat_v,
    cin_v,
    tw1_v,
    tw2_v,
    emb_v,
    c1_v,
    c2_v,
    qkv_v,
    proj_v,
    cout_v,
    load_sem,
    lat_f,
    lat_b,
    xt,
    cin_f,
    cin_w,
    stream,
    hidden,
    block,
    xm,
    xr,
    kr,
    nr,
    wqkv,
    wproj,
    projected,
    pairs,
    bias,
    cout_f,
    wout,
    attended,
    rows_st,
    stats,
    edge_raw,
    edge_scaled,
    edge_in,
    edge_next,
    main_out,
    main_in,
    lat_send,
    lat_recv,
    stat_send,
    stat_recv,
    edge_send,
    edge_recv,
    main_send,
    main_recv,
):
    q = lax.axis_index("queue")
    s = lax.axis_index("space")
    up = lax.rem(s + ns - 1, ns)
    down = lax.rem(s + 1, ns)
    ahead = lax.rem(q + 1, nq)
    behind = lax.rem(q + nq - 1, nq)
    ring = ns // 2
    order = sorted(range(1, ns), key=lambda j: -min(j % ring, ring - j % ring))
    first = s == 0
    last = s == ns - 1

    barrier = pltpu.get_barrier_semaphore()

    def greet(j, _):
        peer = lax.rem(s + j, ns)
        pl.semaphore_signal(barrier, inc=1, device_id=(q, peer), device_id_type=MESH)
        return 0

    lax.fori_loop(1, ns, greet, 0)
    for peer in (up, s, down):
        pl.semaphore_signal(barrier, inc=1, device_id=(behind, peer), device_id_type=MESH)

    loads = [
        pltpu.make_async_copy(src, dst, load_sem.at[i])
        for i, (src, dst) in enumerate(
            (
                (lat_hbm, lat_v),
                (cin_hbm, cin_v),
                (tw1_hbm, tw1_v),
                (tw2_hbm, tw2_v),
                (emb_hbm, emb_v),
                (c1_hbm, c1_v),
                (c2_hbm, c2_v),
                (qkv_hbm, qkv_v),
                (proj_hbm, proj_v),
                (cout_hbm, cout_v),
                (ts_hbm, ts_ref),
                (map_hbm, map_ref),
            )
        )
    ]
    for load in loads:
        load.start()
    load_lat, load_cin, load_tw1, load_tw2, load_emb, load_c1, load_c2, load_qkv, load_proj, load_cout, load_ts, load_map = loads

    load_lat.wait()
    lat_f[12:16, :] = jnp.zeros((4, CELLS), F32)
    for f in range(FRAMES):
        lat_f[0:12, f * COLS : (f + 1) * COLS] = lat_v[pl.ds(f, 12, stride=FRAMES), :]
    lat_b[1] = lat_f[...].astype(BF)

    pl.semaphore_wait(barrier, ns - 1 + 3)

    lat_down = pltpu.make_async_remote_copy(
        lat_b.at[1], lat_b.at[0], lat_send.at[0], lat_recv.at[0], device_id=(q, down), device_id_type=MESH
    )
    lat_up = pltpu.make_async_remote_copy(
        lat_b.at[1], lat_b.at[2], lat_send.at[1], lat_recv.at[1], device_id=(q, up), device_id_type=MESH
    )
    lat_down.start()
    lat_up.start()

    ci = iota((CH, CH), 0) * 6554 >> 16
    cj = iota((CH, CH), 1) * 6554 >> 16
    pairs[...] = jnp.where(ci == cj, 1.0, 0.0).astype(BF)

    load_cin.wait()
    cin_f[36:40, :] = jnp.zeros((4, CH), F32)
    for a in range(3):
        for b in range(3):
            t = a * 3 + b
            cin_f[t * 4 : t * 4 + 4, :] = cin_v[a, b].astype(F32)

    kk = iota((128, 40), 0)
    jj = iota((128, 40), 1)
    tap_b = jnp.where(kk >= 36, 1, 0) + jnp.where(kk >= 72, 1, 0)
    left = kk - 36 * tap_b
    part = left * 5462 >> 16
    left = left - 12 * part
    chan = left * 21846 >> 16
    row_of = 3 * part + left - 3 * chan

    def place_cin(y, _):
        tap_a = row_of - y
        hit = (tap_a >= 0) & (tap_a < 3) & (jj == (tap_a * 3 + tap_b) * 4 + chan)
        sel = jnp.where(hit, 1.0, 0.0).astype(BF)
        cin_w[y] = dot(sel, cin_f[...].astype(BF)).astype(BF)
        return 0

    lax.fori_loop(0, 7, place_cin, 0)

    xr[:, 192:256] = jnp.zeros((9 * CELLS, 64), BF)

    def shared_passes(which, w):
        for b in range(3):
            for a in range(3):
                kr[which, b, a * REST : (a + 1) * REST, :] = w[a, b, MAIN:CH, 0:MAIN]
            kr[which, b, 3 * REST : 256, :] = jnp.zeros((256 - 3 * REST, MAIN), BF)
        for a in range(3):
            for b in range(3):
                nr[which, a * 256 : (a + 1) * 256, b * REST : (b + 1) * REST] = w[a, b, 0:MAIN, MAIN:CH]
                nr[which, 768 + a * REST : 768 + (a + 1) * REST, b * REST : (b + 1) * REST] = w[
                    a, b, MAIN:CH, MAIN:CH
                ]
        nr[which, :, 3 * REST : 256] = jnp.zeros((1024, 256 - 3 * REST), BF)
        nr[which, 768 + 3 * REST : 1024, :] = jnp.zeros((256 - 3 * REST, 256), BF)

    lat_down.wait_recv()
    lat_up.wait_recv()
    lane = iota((16, CELLS), 1) & (COLS - 1)
    xt[108:128, :] = jnp.zeros((20, CELLS), F32)
    for n in range(3):
        v = lat_b[n].astype(F32)
        if n == 0:
            v = jnp.where(first, 0.0, v)
        if n == 2:
            v = jnp.where(last, 0.0, v)
        shifted = (
            jnp.where(lane == 0, 0.0, pltpu.roll(v, 1, 1)),
            v,
            jnp.where(lane == COLS - 1, 0.0, pltpu.roll(v, CELLS - 1, 1)),
        )
        for b in range(3):
            xt[b * 36 + n * 12 : b * 36 + n * 12 + 12, :] = shifted[b][0:12]
    x_in = xt[...].T.astype(BF)

    def cells(r, n=1):
        return pl.ds(r * CELLS if isinstance(r, int) else pl.multiple_of(r * CELLS, CELLS), n * CELLS)

    def row_stats(r, x):
        m = jnp.sum(x, axis=0, keepdims=True) * (1.0 / CELLS)
        rows_st[0, pl.ds(r, 1), :] = m
        rows_st[1, pl.ds(r, 1), :] = jnp.sum((x - m) ** 2, axis=0, keepdims=True)

    def send_stats(phase):
        m = rows_st[0, 0:ROWS, :]
        mean = jnp.sum(m, axis=0, keepdims=True) * (1.0 / ROWS)
        dev = jnp.sum(rows_st[1, 0:ROWS, :] + CELLS * (m - mean) ** 2, axis=0, keepdims=True)
        stats[phase, s] = jnp.concatenate([mean, dev], axis=0)

        for j in order:
            pltpu.make_async_remote_copy(
                stats.at[phase, s],
                stats.at[phase, s],
                stat_send.at[phase],
                stat_recv.at[phase],
                device_id=(q, lax.rem(s + j, ns)),
                device_id_type=MESH,
            ).start()
        near = dot(jnp.broadcast_to(mean, (16, CH)).astype(BF), pairs[...])
        return near[0:1] * (1.0 / PER_GROUP)

    def take_stats(phase, near):
        pltpu.make_async_copy(
            stats.at[phase, pl.ds(0, ns - 1)], stats.at[phase, pl.ds(0, ns - 1)], stat_recv.at[phase]
        ).wait()
        v = stats[phase]
        d = v - jnp.concatenate([near, jnp.zeros_like(near)], axis=0)
        total = jnp.sum(d, axis=0)
        square = jnp.sum(d * d, axis=0)
        s1 = total[0:1]
        s2 = total[1:2] + (ROWS * CELLS) * square[0:1]
        parts = split3(s1) + split3(s2)
        stacked = jnp.concatenate([p.astype(F32) for p in parts] + [jnp.zeros((10, CH), F32)], axis=0)
        g = dot(stacked.astype(BF), pairs[...])
        off = (g[0:1] + g[1:2] + g[2:3]) * (1.0 / (ns * PER_GROUP))
        spread = (g[3:4] + g[4:5] + g[5:6]) * (1.0 / (ns * PER_GROUP * ROWS * CELLS)) - off * off
        return near + off, lax.rsqrt(jnp.maximum(spread, 0.0) + NORM_EPS)

    def stats_sent(phase):
        pltpu.make_async_copy(
            stats.at[phase, pl.ds(0, ns - 1)], stats.at[phase, pl.ds(0, ns - 1)], stat_send.at[phase]
        ).wait()

    def put_normed(r, y):
        yb = y.astype(BF)
        xm[cells(r), :] = yb[:, 0:MAIN]
        rest = yb[:, MAIN:CH]
        xr[cells(r + 2), 0:REST] = rest
        xr[cells(r + 1), REST : 2 * REST] = rest
        xr[cells(r), 2 * REST : 3 * REST] = rest

    def column(n, width, x):
        return jnp.where((iota((n * CELLS, width), 0) & (COLS - 1)) == x, 0.0, 1.0)

    def conv_rows(which, w, rows):
        n = len(rows)
        size = n * CELLS

        def window(ref, a):
            return jnp.concatenate([ref[cells(y + a), :] for y in rows], axis=0)

        x = jnp.concatenate([window(xm, 0), window(xm, 1), window(xm, 2), window(xr, 2)], axis=1)
        z = [
            dot(
                x,
                jnp.concatenate(
                    [w[0, b, 0:MAIN, 0:MAIN], w[1, b, 0:MAIN, 0:MAIN], w[2, b, 0:MAIN, 0:MAIN], kr[which, b]], axis=0
                ),
            )
            for b in range(3)
        ]
        main = (
            z[1] + column(n, MAIN, 0) * pltpu.roll(z[0], 1, 0) + column(n, MAIN, COLS - 1) * pltpu.roll(z[2], size - 1, 0)
        )
        zr = dot(x, nr[which])
        rest = (
            column(n, REST, 0) * pltpu.roll(zr, 1, 0)[:, 0:REST]
            + zr[:, REST : 2 * REST]
            + column(n, REST, COLS - 1) * pltpu.roll(zr, size - 1, 0)[:, 2 * REST : 3 * REST]
        )
        return main, rest

    def stream_row(y):
        v = dot(x_in, cin_w[y])
        stream[cells(y), :] = v
        return v

    def own_stream(i, _):
        row_stats(i, stream_row(i + 2))
        return 0

    lax.fori_loop(0, ROWS, own_stream, 0)
    near1 = send_stats(0)

    for y in (0, 1, 5, 6):
        stream_row(y)

    load_ts.wait()
    load_map.wait()
    level = ts_ref[map_ref[q]]
    pos = iota((16, CH), 1)
    half = CH // 2
    k = jnp.where(pos < half, pos, pos - half).astype(F32)
    phases = level.astype(F32) * jnp.exp(k * (-math.log(10000.0) / half))
    sinusoid = jnp.where(pos < half, jnp.cos(phases), jnp.sin(phases)).astype(BF)
    load_tw1.wait()
    h = dot(sinusoid, tw1_v[...])
    first_hidden = silu_of_half(0.5 * h).astype(BF)
    load_tw2.wait()
    h = dot(first_hidden, tw2_v[...])
    second = silu_of_half(0.5 * h).astype(BF)
    load_emb.wait()
    bias[...] = dot_nt(second, emb_v[...])[0:1]
    load_c1.wait()
    shared_passes(0, c1_v)

    mean, inv = take_stats(0, near1)
    half_inv = 0.5 * inv

    def norm1(r, _):
        y = silu_of_half((stream[cells(r), :] - mean) * half_inv)
        row = s * ROWS + r - 2
        put_normed(r, jnp.where((row >= 0) & (row < ns * ROWS), y, 0.0))
        return 0

    lax.fori_loop(1, 6, norm1, 0)

    def hidden_rows(rows):
        main, rest = conv_rows(0, c1_v, rows)
        for i, j in enumerate(rows):
            hidden[cells(j), 0:MAIN] = main[i * CELLS : (i + 1) * CELLS] + bias[:, 0:MAIN]
            hidden[cells(j), MAIN:CH] = rest[i * CELLS : (i + 1) * CELLS] + bias[:, MAIN:CH]

    hidden_rows((1, 2, 3))
    for i in range(ROWS):
        row_stats(i, hidden[cells(i + 1), :])
    near2 = send_stats(1)

    norm1(0, 0)
    norm1(6, 0)
    hidden_rows((0, 4))
    load_c2.wait()
    shared_passes(1, c2_v)

    mean2, inv2 = take_stats(1, near2)
    half_inv2 = 0.5 * inv2

    def norm2(r, _):
        y = silu_of_half((hidden[cells(r), :] - mean2) * half_inv2)
        row = s * ROWS + r - 1
        put_normed(r, jnp.where((row >= 0) & (row < ns * ROWS), y, 0.0))
        return 0

    lax.fori_loop(0, 5, norm2, 0)

    main, rest = conv_rows(1, c2_v, (0, 1, 2))
    block[:, 0:MAIN] = stream[cells(2, ROWS), 0:MAIN] + main
    block[:, MAIN:CH] = stream[cells(2, ROWS), MAIN:CH] + rest
    for i in range(ROWS):
        row_stats(i, block[cells(i), :])
    near3 = send_stats(2)

    load_qkv.wait()
    wqkv[:, 0:CH] = qkv_v[:, 0:CH] * jnp.asarray(HEAD_DIM**-0.5, BF)
    wqkv[:, CH:384] = jnp.zeros((CH, 384 - CH), BF)
    wqkv[:, 384:1024] = qkv_v[:, CH : 3 * CH]
    load_proj.wait()
    wproj[0:64, :] = jnp.zeros((64, CH), BF)
    wproj[64:384, :] = proj_v[...]
    load_cout.wait()
    cout_f[36:40, :] = jnp.zeros((4, CH), F32)
    for a in range(3):
        for b in range(3):
            r = (a * 3 + b) * 4
            cout_f[r : r + 4, :] = cout_v[a, b].astype(F32)
    to = iota((144, 40), 0)
    src = iota((144, 40), 1)
    to_b = jnp.where(to >= 48, 1, 0) + jnp.where(to >= 96, 1, 0)
    to_part = to - 48 * to_b >> 4
    to_row = to & 15
    to_c = to_row * 21846 >> 16
    to_y = to_row - 3 * to_c + jnp.where(to_part == 1, ROWS, 0) - jnp.where(to_part == 2, ROWS, 0)
    for i in range(ROWS):
        tap = i - to_y + 1
        hit = (tap >= 0) & (tap < 3) & (to_row < 12) & (src == (tap * 3 + to_b) * 4 + to_c)
        wout[i] = dot(jnp.where(hit, 1.0, 0.0).astype(BF), cout_f[...].astype(BF)).astype(BF)

    step_of = iota((8, 128), 0) * 128 + iota((8, 128), 1)
    lo, hi = 0.00085**0.5, 0.012**0.5
    beta = (lo + step_of.astype(F32) * ((hi - lo) / 999.0)) ** 2

    def alpha(t):
        v = jnp.where(step_of <= t, 1.0 - beta, 1.0)
        for sh in (64, 32, 16, 8, 4, 2, 1):
            v = v * pltpu.roll(v, sh, 1)
        for sh in (4, 2, 1):
            v = v * pltpu.roll(v, sh, 0)
        return v[0:1, 0:1]

    alpha_now = alpha(level)
    alpha_next = alpha(level - STEP)
    keep = jnp.sqrt(alpha_next / alpha_now)
    gain = jnp.sqrt(1.0 - alpha_next) - keep * jnp.sqrt(1.0 - alpha_now)

    mean3, inv3 = take_stats(2, near3)

    same = ((iota((CELLS, CELLS), 0) ^ iota((CELLS, CELLS), 1)) & (COLS - 1)) == 0
    low_half = iota((CELLS, 128), 1) < HEAD_DIM

    projected[...] = dot(((block[...] - mean3) * inv3).astype(BF), wqkv[...]).astype(BF)

    def attend_row(i, _):
        row = cells(i)
        ones = jnp.ones((CELLS, 128), BF)

        def head(h):
            qt = projected[row, h // 2 * 128 : h // 2 * 128 + 128]
            if h < HEADS - 1:
                qt = jnp.where(low_half if h % 2 == 0 else jnp.logical_not(low_half), qt, jnp.zeros_like(qt))
            kt = projected[row, 384 + h // 2 * 128 : 512 + h // 2 * 128]
            vt = projected[row, 640 + (h + 1) // 2 * 128 : 768 + (h + 1) // 2 * 128]
            sc = jnp.where(same, dot_nt(qt, kt), -1e30)
            p = jnp.exp(sc - jnp.max(sc, axis=1, keepdims=True)).astype(BF)
            o = dot(p, jnp.concatenate([vt, ones], axis=1))
            return o[:, 0:128] / o[:, 128:256]

        attended[row, 0:128] = jnp.where(low_half, 0.0, head(0)).astype(BF)
        attended[row, 128:256] = jnp.where(low_half, head(1), head(2)).astype(BF)
        attended[row, 256:384] = jnp.where(low_half, head(3), head(4)).astype(BF)
        return 0

    lax.fori_loop(0, ROWS, attend_row, 0)
    block[...] += dot(attended[...], wproj[...])
    for i in range(ROWS):
        row_stats(i, block[cells(i), :])
    near4 = send_stats(3)
    mean4, inv4 = take_stats(3, near4)
    half_inv4 = 0.5 * inv4

    z = jnp.zeros((144, CELLS), F32)
    for i in range(ROWS):
        z = z + dot_nt(wout[i], silu_of_half((block[cells(i), :] - mean4) * half_inv4).astype(BF))
    lane = iota((48, CELLS), 1) & (COLS - 1)
    sums = (
        z[48:96]
        + jnp.where(lane == 0, 0.0, pltpu.roll(z[0:48], 1, 1))
        + jnp.where(lane == COLS - 1, 0.0, pltpu.roll(z[96:144], CELLS - 1, 1))
    )
    own = sums[0:16]
    for side in range(2):
        edge_raw[side] = sums[16 + 16 * side : 32 + 16 * side]
        edge_scaled[side] = gain * sums[16 + 16 * side : 32 + 16 * side]
    sends = []
    for side, peer in ((0, down), (1, up)):
        sends.append(
            pltpu.make_async_remote_copy(
                edge_scaled.at[side],
                edge_next.at[side],
                edge_send.at[side],
                edge_recv.at[side],
                device_id=(ahead, peer),
                device_id_type=MESH,
            )
        )
        sends.append(
            pltpu.make_async_remote_copy(
                edge_raw.at[side],
                edge_in.at[side],
                edge_send.at[2 + side],
                edge_recv.at[2 + side],
                device_id=(q, peer),
                device_id_type=MESH,
            )
        )
    for send in sends:
        send.start()
    main_out[...] = keep * lat_f[...] + gain * own
    main_send_copy = pltpu.make_async_remote_copy(
        main_out, main_in, main_send, main_recv, device_id=(ahead, s), device_id_type=MESH
    )
    main_send_copy.start()

    def put(out, v):
        for f in range(FRAMES):
            out[pl.ds(f, 12, stride=FRAMES), :] = v[0:12, f * COLS : (f + 1) * COLS]

    sends[1].wait_recv()
    sends[3].wait_recv()
    put(noise_ref, own + jnp.where(first, 0.0, edge_in[0]) + jnp.where(last, 0.0, edge_in[1]))
    main_send_copy.wait_recv()
    sends[0].wait_recv()
    sends[2].wait_recv()
    put(next_ref, main_in[...] + jnp.where(first, 0.0, edge_next[0]) + jnp.where(last, 0.0, edge_next[1]))

    lat_down.wait_send()
    lat_up.wait_send()
    for phase in range(4):
        stats_sent(phase)
    for send in sends:
        send.wait_send()
    main_send_copy.wait_send()


def per_device(
    nq,
    ns,
    latents,
    fresh_noise,
    timesteps,
    queue_map,
    conv_in_w,
    time_w1,
    time_w2,
    emb_w,
    conv1_w,
    conv2_w,
    qkv_w,
    proj_w,
    conv_out_w,
):
    hbm = pl.BlockSpec(memory_space=pltpu.HBM)
    vmem = pl.BlockSpec(memory_space=pltpu.VMEM)
    latents = jnp.transpose(latents[0], (0, 2, 1, 3)).reshape(4 * ROWS * FRAMES, COLS)
    emb_t = emb_w.T
    out_t = jnp.swapaxes(conv_out_w, 2, 3)
    weights = (conv_in_w, time_w1, time_w2, emb_t, conv1_w, conv2_w, qkv_w, proj_w, out_t)
    DMA = pltpu.SemaphoreType.DMA
    operands = [
        pltpu.with_memory_space_constraint(v, pltpu.HBM) for v in (timesteps, queue_map, latents, *weights)
    ]
    noise, nxt = pl.pallas_call(
        functools.partial(kernel, nq, ns),
        out_shape=(
            jax.ShapeDtypeStruct((4 * ROWS * FRAMES, COLS), F32),
            jax.ShapeDtypeStruct((4 * ROWS * FRAMES, COLS), F32),
        ),
        in_specs=[hbm] * len(operands),
        out_specs=(vmem, vmem),
        scratch_shapes=[pltpu.SMEM(timesteps.shape, jnp.int32), pltpu.SMEM(queue_map.shape, jnp.int32)]
        + [pltpu.VMEM(latents.shape, F32)]
        + [pltpu.VMEM(w.shape, BF) for w in weights]
        + [
            DMA((len(operands),)),
            pltpu.VMEM((16, CELLS), F32),
            pltpu.VMEM((3, 16, CELLS), BF),
            pltpu.VMEM((128, CELLS), F32),
            pltpu.VMEM((40, CH), F32),
            pltpu.VMEM((7, 128, CH), BF),
            pltpu.VMEM((7 * CELLS, CH), F32),
            pltpu.VMEM((5 * CELLS, CH), F32),
            pltpu.VMEM((3 * CELLS, CH), F32),
            pltpu.VMEM((7 * CELLS, MAIN), BF),
            pltpu.VMEM((9 * CELLS, 256), BF),
            pltpu.VMEM((2, 3, 256, MAIN), BF),
            pltpu.VMEM((2, 1024, 256), BF),
            pltpu.VMEM((CH, 1024), BF),
            pltpu.VMEM((384, CH), BF),
            pltpu.VMEM((ROWS * CELLS, 1024), BF),
            pltpu.VMEM((CH, CH), BF),
            pltpu.VMEM((1, CH), F32),
            pltpu.VMEM((40, CH), F32),
            pltpu.VMEM((3, 144, CH), BF),
            pltpu.VMEM((ROWS * CELLS, 384), BF),
            pltpu.VMEM((2, 8, CH), F32),
            pltpu.VMEM((4, ns, 2, CH), F32),
            pltpu.VMEM((2, 16, CELLS), F32),
            pltpu.VMEM((2, 16, CELLS), F32),
            pltpu.VMEM((2, 16, CELLS), F32),
            pltpu.VMEM((2, 16, CELLS), F32),
            pltpu.VMEM((16, CELLS), F32),
            pltpu.VMEM((16, CELLS), F32),
            DMA((2,)),
            DMA((2,)),
            DMA((4,)),
            DMA((4,)),
            DMA((4,)),
            DMA((4,)),
            DMA,
            DMA,
        ],
        compiler_params=pltpu.CompilerParams(
            collective_id=0, has_side_effects=True, vmem_limit_bytes=44 * 1024 * 1024
        ),
        cost_estimate=pl.CostEstimate(flops=10**10, bytes_accessed=10**7, transcendentals=10**6),
    )(*operands)

    def as_frames(v):
        return jnp.transpose(v.reshape(4, ROWS, FRAMES, COLS), (0, 2, 1, 3))

    next_queue = jnp.where(lax.axis_index("queue") == 0, fresh_noise, as_frames(nxt))
    return as_frames(noise)[None], next_queue[None]


def solution(mesh):
    nq, ns = mesh.shape["queue"], mesh.shape["space"]
    rows = P("queue", None, None, "space", None)
    return jax.shard_map(
        functools.partial(per_device, nq, ns),
        mesh=mesh,
        in_specs=(rows, P(None, None, "space", None)) + (P(),) * 11,
        out_specs=(rows, rows),
        check_vma=False,
    )
```

```python
import functools
import math

import jax
import jax.numpy as jnp
from jax import lax
from jax.experimental import pallas as pl
from jax.experimental.pallas import tpu as pltpu
from jax.sharding import PartitionSpec as P

GROUPS = 32
HEAD_DIM = 64
STEP = 50
NORM_EPS = 1e-05
MESH = pl.DeviceIdType.MESH

CH = 320
FRAMES = 16
COLS = 16
ROWS = 3
CELLS = FRAMES * COLS
PER_GROUP = CH // GROUPS
HEADS = CH // HEAD_DIM
MAIN = 256
REST = CH - MAIN
BF = jnp.bfloat16
F32 = jnp.float32


def dot(a, b):
    return jnp.dot(a, b, preferred_element_type=F32)


def dot_nt(a, b):
    return lax.dot_general(a, b, (((1,), (1,)), ((), ())), preferred_element_type=F32)


def silu_of_half(h):
    return h + h * jnp.tanh(h)


def iota(shape, dim):
    return lax.broadcasted_iota(jnp.int32, shape, dim)


def split3(v):
    hi = v.astype(BF)
    left = v - hi.astype(F32)
    mid = left.astype(BF)
    return hi, mid, (left - mid.astype(F32)).astype(BF)


def stack(parts):
    rows = [p.astype(F32) for p in parts]
    return jnp.concatenate(rows + [jnp.zeros((16 - len(rows), rows[0].shape[1]), F32)], axis=0).astype(BF)


def kernel(
    nq,
    ns,
    ts_hbm,
    map_hbm,
    lat_hbm,
    cin_hbm,
    tw1_hbm,
    tw2_hbm,
    emb_hbm,
    c1_hbm,
    c2_hbm,
    qkv_hbm,
    proj_hbm,
    cout_hbm,
    noise_ref,
    next_ref,
    ts_ref,
    map_ref,
    lat_v,
    cin_v,
    tw1_v,
    tw2_v,
    emb_v,
    c1_v,
    c2_v,
    qkv_v,
    proj_v,
    cout_v,
    load_sem,
    lat_f,
    lat_b,
    shifted,
    cin_f,
    cin_w,
    stream,
    hidden,
    block,
    xm,
    xr,
    kr,
    nr,
    wqkv,
    wproj,
    projected,
    pairs,
    bias,
    cout_f,
    wout,
    attended,
    rows_st,
    stats,
    edge_raw,
    edge_scaled,
    edge_in,
    edge_next,
    main_out,
    main_in,
    lat_send,
    lat_recv,
    stat_send,
    stat_recv,
    edge_send,
    edge_recv,
    main_send,
    main_recv,
):
    q = lax.axis_index("queue")
    s = lax.axis_index("space")
    up = lax.rem(s + ns - 1, ns)
    down = lax.rem(s + 1, ns)
    ahead = lax.rem(q + 1, nq)
    behind = lax.rem(q + nq - 1, nq)
    ring = ns // 2
    order = sorted(range(1, ns), key=lambda j: -min(j % ring, ring - j % ring))
    first = s == 0
    last = s == ns - 1

    def cells(r, n=1):
        return pl.ds(r * CELLS if isinstance(r, int) else pl.multiple_of(r * CELLS, CELLS), n * CELLS)

    barrier = pltpu.get_barrier_semaphore()

    def greet(j, _):
        peer = lax.rem(s + j, ns)
        pl.semaphore_signal(barrier, inc=1, device_id=(q, peer), device_id_type=MESH)
        return 0

    lax.fori_loop(1, ns, greet, 0)
    for peer in (up, s, down):
        pl.semaphore_signal(barrier, inc=1, device_id=(behind, peer), device_id_type=MESH)

    loads = [
        pltpu.make_async_copy(src, dst, load_sem.at[i])
        for i, (src, dst) in enumerate(
            (
                (lat_hbm, lat_v),
                (cin_hbm, cin_v),
                (tw1_hbm, tw1_v),
                (tw2_hbm, tw2_v),
                (emb_hbm, emb_v),
                (c1_hbm, c1_v),
                (c2_hbm, c2_v),
                (qkv_hbm, qkv_v),
                (proj_hbm, proj_v),
                (cout_hbm, cout_v),
                (ts_hbm, ts_ref),
                (map_hbm, map_ref),
            )
        )
    ]
    for load in loads:
        load.start()
    load_lat, load_cin, load_tw1, load_tw2, load_emb, load_c1, load_c2, load_qkv, load_proj, load_cout, load_ts, load_map = loads

    load_lat.wait()
    lat_f[12:16, :] = jnp.where(iota((4, CELLS), 0) == 0, 1.0, 0.0)
    for f in range(FRAMES):
        lat_f[0:12, f * COLS : (f + 1) * COLS] = lat_v[pl.ds(f, 12, stride=FRAMES), :]
    own_rows = pl.ds(pl.multiple_of((s + 1) * 16, 16), 16)
    lat_b[own_rows, :] = lat_f[...].astype(BF)
    lat_b[0:16, :] = jnp.zeros((16, CELLS), BF)
    lat_b[(ns + 1) * 16 :, :] = jnp.zeros((16, CELLS), BF)

    pl.semaphore_wait(barrier, ns - 1 + 3)

    lat_sends = {
        j: pltpu.make_async_remote_copy(
            lat_b.at[own_rows],
            lat_b.at[own_rows],
            lat_send,
            lat_recv.at[0 if j == 1 else 1 if j == ns - 1 else 2],
            device_id=(q, lax.rem(s + j, ns)),
            device_id_type=MESH,
        )
        for j in order
    }
    for j in order:
        lat_sends[j].start()

    ci = iota((CH, CH), 0) * 6554 >> 16
    cj = iota((CH, CH), 1) * 6554 >> 16
    pairs[...] = jnp.where(ci == cj, 1.0, 0.0).astype(BF)

    load_cin.wait()
    cin_f[36:40, :] = jnp.zeros((4, CH), F32)
    for a in range(3):
        for b in range(3):
            t = a * 3 + b
            cin_f[t * 4 : t * 4 + 4, :] = cin_v[a, b].astype(F32)

    kk = iota((144, 40), 0)
    jj = iota((144, 40), 1)
    tap_b = jnp.where(kk >= 48, 1, 0) + jnp.where(kk >= 96, 1, 0)
    left = kk - 48 * tap_b
    in_block = left & 15
    chan = in_block * 21846 >> 16
    row_of = 3 * (left >> 4) + in_block - 3 * chan

    def place_cin(y, _):
        tap_a = row_of - y
        hit = (tap_a >= 0) & (tap_a < 3) & (in_block < 12) & (jj == (tap_a * 3 + tap_b) * 4 + chan)
        sel = jnp.where(hit, 1.0, 0.0).astype(BF)
        cin_w[y] = dot(sel, cin_f[...].astype(BF)).astype(BF)
        return 0

    lax.fori_loop(0, 7, place_cin, 0)

    xr[:, 192:256] = jnp.zeros((9 * CELLS, 64), BF)

    def shared_passes(which, w):
        for b in range(3):
            for a in range(3):
                kr[which, b, a * REST : (a + 1) * REST, :] = w[a, b, MAIN:CH, 0:MAIN]
            kr[which, b, 3 * REST : 256, :] = jnp.zeros((256 - 3 * REST, MAIN), BF)
        for a in range(3):
            for b in range(3):
                nr[which, a * 256 : (a + 1) * 256, b * REST : (b + 1) * REST] = w[a, b, 0:MAIN, MAIN:CH]
                nr[which, 768 + a * REST : 768 + (a + 1) * REST, b * REST : (b + 1) * REST] = w[
                    a, b, MAIN:CH, MAIN:CH
                ]
        nr[which, :, 3 * REST : 256] = jnp.zeros((1024, 256 - 3 * REST), BF)
        nr[which, 768 + 3 * REST : 1024, :] = jnp.zeros((256 - 3 * REST, 256), BF)

    def shift_blocks(start, n):
        rows = pl.ds(start if isinstance(start, int) else pl.multiple_of(start * 16, 16), n * 16)
        v = lat_b[rows, :].astype(F32)
        lane = iota((n * 16, CELLS), 1) & (COLS - 1)
        shifted[0, rows, :] = jnp.where(lane == 0, 0.0, pltpu.roll(v, 1, 1)).astype(BF)
        shifted[1, rows, :] = lat_b[rows, :]
        shifted[2, rows, :] = jnp.where(lane == COLS - 1, 0.0, pltpu.roll(v, CELLS - 1, 1)).astype(BF)

    lat_sends[1].wait_recv()
    lat_sends[ns - 1].wait_recv()
    shift_blocks(s, 3)
    window = pl.ds(pl.multiple_of(s * 16, 16), 48)
    x_in = jnp.concatenate([shifted[b, window, :] for b in range(3)], axis=0).astype(F32).T.astype(BF)

    for y in range(7):
        stream[cells(y), :] = dot(x_in, cin_w[y])

    def row_stats(r, x):
        m = jnp.sum(x, axis=0, keepdims=True) * (1.0 / CELLS)
        rows_st[0, pl.ds(r, 1), :] = m
        rows_st[1, pl.ds(r, 1), :] = jnp.sum((x - m) ** 2, axis=0, keepdims=True)

    def send_stats(phase):
        m = rows_st[0, 0:ROWS, :]
        mean = jnp.sum(m, axis=0, keepdims=True) * (1.0 / ROWS)
        dev = jnp.sum(rows_st[1, 0:ROWS, :] + CELLS * (m - mean) ** 2, axis=0, keepdims=True)
        stats[phase, s] = jnp.concatenate([mean, dev], axis=0)

        for j in order:
            pltpu.make_async_remote_copy(
                stats.at[phase, s],
                stats.at[phase, s],
                stat_send.at[phase],
                stat_recv.at[phase],
                device_id=(q, lax.rem(s + j, ns)),
                device_id_type=MESH,
            ).start()
        near = dot(jnp.broadcast_to(mean, (16, CH)).astype(BF), pairs[...])
        return near[0:1] * (1.0 / PER_GROUP)

    def take_stats(phase, near, shift=0.0):
        pltpu.make_async_copy(
            stats.at[phase, pl.ds(0, ns - 1)], stats.at[phase, pl.ds(0, ns - 1)], stat_recv.at[phase]
        ).wait()
        v = stats[phase]
        d = v - jnp.concatenate([near - shift, jnp.zeros_like(near)], axis=0)
        total = jnp.sum(d, axis=0)
        square = jnp.sum(d * d, axis=0)
        s1 = total[0:1]
        s2 = total[1:2] + (ROWS * CELLS) * square[0:1]
        parts = split3(s1) + split3(s2)
        g = dot(stack(parts), pairs[...])
        off = (g[0:1] + g[1:2] + g[2:3]) * (1.0 / (ns * PER_GROUP))
        spread = (g[3:4] + g[4:5] + g[5:6]) * (1.0 / (ns * PER_GROUP * ROWS * CELLS)) - off * off
        return near + off, lax.rsqrt(jnp.maximum(spread, 0.0) + NORM_EPS)

    def stats_sent(phase):
        pltpu.make_async_copy(
            stats.at[phase, pl.ds(0, ns - 1)], stats.at[phase, pl.ds(0, ns - 1)], stat_send.at[phase]
        ).wait()

    def put_normed(r, y):
        yb = y.astype(BF)
        xm[cells(r), :] = yb[:, 0:MAIN]
        rest = yb[:, MAIN:CH]
        xr[cells(r + 2), 0:REST] = rest
        xr[cells(r + 1), REST : 2 * REST] = rest
        xr[cells(r), 2 * REST : 3 * REST] = rest

    def column(n, width, x):
        return jnp.where((iota((n * CELLS, width), 0) & (COLS - 1)) == x, 0.0, 1.0)

    def conv_rows(which, w, rows):
        n = len(rows)
        size = n * CELLS

        def window(ref, a):
            return jnp.concatenate([ref[cells(y + a), :] for y in rows], axis=0)

        x = jnp.concatenate([window(xm, 0), window(xm, 1), window(xm, 2), window(xr, 2)], axis=1)
        z = [
            dot(
                x,
                jnp.concatenate(
                    [w[0, b, 0:MAIN, 0:MAIN], w[1, b, 0:MAIN, 0:MAIN], w[2, b, 0:MAIN, 0:MAIN], kr[which, b]], axis=0
                ),
            )
            for b in range(3)
        ]
        main = (
            z[1] + column(n, MAIN, 0) * pltpu.roll(z[0], 1, 0) + column(n, MAIN, COLS - 1) * pltpu.roll(z[2], size - 1, 0)
        )
        zr = dot(x, nr[which])
        rest = (
            column(n, REST, 0) * pltpu.roll(zr, 1, 0)[:, 0:REST]
            + zr[:, REST : 2 * REST]
            + column(n, REST, COLS - 1) * pltpu.roll(zr, size - 1, 0)[:, 2 * REST : 3 * REST]
        )
        return main, rest

    load_c1.wait()
    shared_passes(0, c1_v)

    pltpu.make_async_copy(lat_b.at[pl.ds(0, (ns - 3) * 16)], lat_b.at[pl.ds(0, (ns - 3) * 16)], lat_recv.at[2]).wait()
    shift_blocks(0, ns + 2)
    every = jnp.concatenate(
        [jnp.concatenate([shifted[b, n * 16 : n * 16 + 48, :] for b in range(3)], axis=0) for n in range(ns)], axis=1
    )
    products = jnp.concatenate(split3(dot_nt(every, every)), axis=0)
    first_sum = jnp.zeros((1, CH), F32)
    second_sum = jnp.zeros((1, CH), F32)
    for y in (2, 3, 4):
        w = cin_w[y]
        g = dot(products, w)
        g = g[0:144] + g[144:288] + g[288:432]
        first_sum = first_sum + g[76:77]
        second_sum = second_sum + jnp.sum(w.astype(F32) * g, axis=0, keepdims=True)
    per_cell = 1.0 / (ns * ROWS * CELLS * PER_GROUP)
    g = dot(stack(split3(first_sum) + split3(second_sum)), pairs[...])
    mean = (g[0:1] + g[1:2] + g[2:3]) * per_cell
    spread = (g[3:4] + g[4:5] + g[5:6]) * per_cell - mean * mean
    inv = lax.rsqrt(jnp.maximum(spread, 0.0) + NORM_EPS)
    half_inv = 0.5 * inv

    def norm1(r, _):
        y = silu_of_half((stream[cells(r), :] - mean) * half_inv)
        row = s * ROWS + r - 2
        put_normed(r, jnp.where((row >= 0) & (row < ns * ROWS), y, 0.0))
        return 0

    lax.fori_loop(1, 6, norm1, 0)

    def hidden_rows(rows):
        main, rest = conv_rows(0, c1_v, rows)
        for i, j in enumerate(rows):
            hidden[cells(j), 0:MAIN] = main[i * CELLS : (i + 1) * CELLS]
            hidden[cells(j), MAIN:CH] = rest[i * CELLS : (i + 1) * CELLS]

    hidden_rows((1, 2, 3))
    for i in range(ROWS):
        row_stats(i, hidden[cells(i + 1), :])
    near2 = send_stats(0)

    norm1(0, 0)
    norm1(6, 0)
    hidden_rows((0, 4))

    load_ts.wait()
    load_map.wait()
    level = ts_ref[map_ref[q]]
    pos = iota((16, CH), 1)
    half = CH // 2
    k = jnp.where(pos < half, pos, pos - half).astype(F32)
    phases = level.astype(F32) * jnp.exp(k * (-math.log(10000.0) / half))
    sinusoid = jnp.where(pos < half, jnp.cos(phases), jnp.sin(phases)).astype(BF)
    load_tw1.wait()
    h = dot(sinusoid, tw1_v[...])
    first_hidden = silu_of_half(0.5 * h).astype(BF)
    load_tw2.wait()
    h = dot(first_hidden, tw2_v[...])
    second = silu_of_half(0.5 * h).astype(BF)
    load_emb.wait()
    bias[...] = dot_nt(second, emb_v[...])[0:1]
    load_c2.wait()
    shared_passes(1, c2_v)

    mean2, inv2 = take_stats(0, near2, bias[...])
    mean2 = mean2 - bias[...]
    half_inv2 = 0.5 * inv2

    def norm2(r, _):
        y = silu_of_half((hidden[cells(r), :] - mean2) * half_inv2)
        row = s * ROWS + r - 1
        put_normed(r, jnp.where((row >= 0) & (row < ns * ROWS), y, 0.0))
        return 0

    lax.fori_loop(0, 5, norm2, 0)

    main, rest = conv_rows(1, c2_v, (0, 1, 2))
    block[:, 0:MAIN] = stream[cells(2, ROWS), 0:MAIN] + main
    block[:, MAIN:CH] = stream[cells(2, ROWS), MAIN:CH] + rest
    for i in range(ROWS):
        row_stats(i, block[cells(i), :])
    near3 = send_stats(1)

    load_qkv.wait()
    wqkv[:, 0:CH] = qkv_v[:, 0:CH] * jnp.asarray(HEAD_DIM**-0.5, BF)
    wqkv[:, CH:384] = jnp.zeros((CH, 384 - CH), BF)
    wqkv[:, 384:1024] = qkv_v[:, CH : 3 * CH]
    load_proj.wait()
    wproj[0:64, :] = jnp.zeros((64, CH), BF)
    wproj[64:384, :] = proj_v[...]
    load_cout.wait()
    cout_f[36:40, :] = jnp.zeros((4, CH), F32)
    for a in range(3):
        for b in range(3):
            r = (a * 3 + b) * 4
            cout_f[r : r + 4, :] = cout_v[a, b].astype(F32)
    to = iota((144, 40), 0)
    src = iota((144, 40), 1)
    to_b = jnp.where(to >= 48, 1, 0) + jnp.where(to >= 96, 1, 0)
    to_part = to - 48 * to_b >> 4
    to_row = to & 15
    to_c = to_row * 21846 >> 16
    to_y = to_row - 3 * to_c + jnp.where(to_part == 1, ROWS, 0) - jnp.where(to_part == 2, ROWS, 0)
    for i in range(ROWS):
        tap = i - to_y + 1
        hit = (tap >= 0) & (tap < 3) & (to_row < 12) & (src == (tap * 3 + to_b) * 4 + to_c)
        wout[i] = dot(jnp.where(hit, 1.0, 0.0).astype(BF), cout_f[...].astype(BF)).astype(BF)

    step_of = iota((8, 128), 0) * 128 + iota((8, 128), 1)
    lo, hi = 0.00085**0.5, 0.012**0.5
    beta = (lo + step_of.astype(F32) * ((hi - lo) / 999.0)) ** 2

    def alpha(t):
        v = jnp.where(step_of <= t, 1.0 - beta, 1.0)
        for sh in (64, 32, 16, 8, 4, 2, 1):
            v = v * pltpu.roll(v, sh, 1)
        for sh in (4, 2, 1):
            v = v * pltpu.roll(v, sh, 0)
        return v[0:1, 0:1]

    alpha_now = alpha(level)
    alpha_next = alpha(level - STEP)
    keep = jnp.sqrt(alpha_next / alpha_now)
    gain = jnp.sqrt(1.0 - alpha_next) - keep * jnp.sqrt(1.0 - alpha_now)

    mean3, inv3 = take_stats(1, near3)

    same = ((iota((CELLS, CELLS), 0) ^ iota((CELLS, CELLS), 1)) & (COLS - 1)) == 0
    low_half = iota((CELLS, 128), 1) < HEAD_DIM

    projected[...] = dot(((block[...] - mean3) * inv3).astype(BF), wqkv[...]).astype(BF)

    def attend_row(i, _):
        row = cells(i)
        ones = jnp.ones((CELLS, 128), BF)

        def head(h):
            qt = projected[row, h // 2 * 128 : h // 2 * 128 + 128]
            if h < HEADS - 1:
                qt = jnp.where(low_half if h % 2 == 0 else jnp.logical_not(low_half), qt, jnp.zeros_like(qt))
            kt = projected[row, 384 + h // 2 * 128 : 512 + h // 2 * 128]
            vt = projected[row, 640 + (h + 1) // 2 * 128 : 768 + (h + 1) // 2 * 128]
            sc = jnp.where(same, dot_nt(qt, kt), -1e30)
            p = jnp.exp(sc - jnp.max(sc, axis=1, keepdims=True)).astype(BF)
            o = dot(p, jnp.concatenate([vt, ones], axis=1))
            return o[:, 0:128] / o[:, 128:256]

        attended[row, 0:128] = jnp.where(low_half, 0.0, head(0)).astype(BF)
        attended[row, 128:256] = jnp.where(low_half, head(1), head(2)).astype(BF)
        attended[row, 256:384] = jnp.where(low_half, head(3), head(4)).astype(BF)
        return 0

    lax.fori_loop(0, ROWS, attend_row, 0)
    block[...] += dot(attended[...], wproj[...])
    for i in range(ROWS):
        row_stats(i, block[cells(i), :])
    near4 = send_stats(2)
    mean4, inv4 = take_stats(2, near4)
    half_inv4 = 0.5 * inv4

    z = jnp.zeros((144, CELLS), F32)
    for i in range(ROWS):
        z = z + dot_nt(wout[i], silu_of_half((block[cells(i), :] - mean4) * half_inv4).astype(BF))
    lane = iota((48, CELLS), 1) & (COLS - 1)
    sums = (
        z[48:96]
        + jnp.where(lane == 0, 0.0, pltpu.roll(z[0:48], 1, 1))
        + jnp.where(lane == COLS - 1, 0.0, pltpu.roll(z[96:144], CELLS - 1, 1))
    )
    own = sums[0:16]
    for side in range(2):
        edge_raw[side] = sums[16 + 16 * side : 32 + 16 * side]
        edge_scaled[side] = gain * sums[16 + 16 * side : 32 + 16 * side]
    sends = []
    for side, peer in ((0, down), (1, up)):
        sends.append(
            pltpu.make_async_remote_copy(
                edge_scaled.at[side],
                edge_next.at[side],
                edge_send.at[side],
                edge_recv.at[side],
                device_id=(ahead, peer),
                device_id_type=MESH,
            )
        )
        sends.append(
            pltpu.make_async_remote_copy(
                edge_raw.at[side],
                edge_in.at[side],
                edge_send.at[2 + side],
                edge_recv.at[2 + side],
                device_id=(q, peer),
                device_id_type=MESH,
            )
        )
    for send in sends:
        send.start()
    main_out[...] = keep * lat_f[...] + gain * own
    main_send_copy = pltpu.make_async_remote_copy(
        main_out, main_in, main_send, main_recv, device_id=(ahead, s), device_id_type=MESH
    )
    main_send_copy.start()

    def put(out, v):
        for f in range(FRAMES):
            out[pl.ds(f, 12, stride=FRAMES), :] = v[0:12, f * COLS : (f + 1) * COLS]

    sends[1].wait_recv()
    sends[3].wait_recv()
    put(noise_ref, own + jnp.where(first, 0.0, edge_in[0]) + jnp.where(last, 0.0, edge_in[1]))
    main_send_copy.wait_recv()
    sends[0].wait_recv()
    sends[2].wait_recv()
    put(next_ref, main_in[...] + jnp.where(first, 0.0, edge_next[0]) + jnp.where(last, 0.0, edge_next[1]))

    pltpu.make_async_copy(lat_b.at[pl.ds(0, (ns - 1) * 16)], lat_b.at[pl.ds(0, (ns - 1) * 16)], lat_send).wait()
    for phase in range(3):
        stats_sent(phase)
    for send in sends:
        send.wait_send()
    main_send_copy.wait_send()


def per_device(
    nq,
    ns,
    latents,
    fresh_noise,
    timesteps,
    queue_map,
    conv_in_w,
    time_w1,
    time_w2,
    emb_w,
    conv1_w,
    conv2_w,
    qkv_w,
    proj_w,
    conv_out_w,
):
    hbm = pl.BlockSpec(memory_space=pltpu.HBM)
    vmem = pl.BlockSpec(memory_space=pltpu.VMEM)
    latents = jnp.transpose(latents[0], (0, 2, 1, 3)).reshape(4 * ROWS * FRAMES, COLS)
    emb_t = emb_w.T
    out_t = jnp.swapaxes(conv_out_w, 2, 3)
    weights = (conv_in_w, time_w1, time_w2, emb_t, conv1_w, conv2_w, qkv_w, proj_w, out_t)
    DMA = pltpu.SemaphoreType.DMA
    operands = [
        pltpu.with_memory_space_constraint(v, pltpu.HBM) for v in (timesteps, queue_map, latents, *weights)
    ]
    noise, nxt = pl.pallas_call(
        functools.partial(kernel, nq, ns),
        out_shape=(
            jax.ShapeDtypeStruct((4 * ROWS * FRAMES, COLS), F32),
            jax.ShapeDtypeStruct((4 * ROWS * FRAMES, COLS), F32),
        ),
        in_specs=[hbm] * len(operands),
        out_specs=(vmem, vmem),
        scratch_shapes=[pltpu.SMEM(timesteps.shape, jnp.int32), pltpu.SMEM(queue_map.shape, jnp.int32)]
        + [pltpu.VMEM(latents.shape, F32)]
        + [pltpu.VMEM(w.shape, BF) for w in weights]
        + [
            DMA((len(operands),)),
            pltpu.VMEM((16, CELLS), F32),
            pltpu.VMEM(((ns + 2) * 16, CELLS), BF),
            pltpu.VMEM((3, (ns + 2) * 16, CELLS), BF),
            pltpu.VMEM((40, CH), F32),
            pltpu.VMEM((7, 144, CH), BF),
            pltpu.VMEM((7 * CELLS, CH), F32),
            pltpu.VMEM((5 * CELLS, CH), F32),
            pltpu.VMEM((3 * CELLS, CH), F32),
            pltpu.VMEM((7 * CELLS, MAIN), BF),
            pltpu.VMEM((9 * CELLS, 256), BF),
            pltpu.VMEM((2, 3, 256, MAIN), BF),
            pltpu.VMEM((2, 1024, 256), BF),
            pltpu.VMEM((CH, 1024), BF),
            pltpu.VMEM((384, CH), BF),
            pltpu.VMEM((ROWS * CELLS, 1024), BF),
            pltpu.VMEM((CH, CH), BF),
            pltpu.VMEM((1, CH), F32),
            pltpu.VMEM((40, CH), F32),
            pltpu.VMEM((3, 144, CH), BF),
            pltpu.VMEM((ROWS * CELLS, 384), BF),
            pltpu.VMEM((2, 8, CH), F32),
            pltpu.VMEM((3, ns, 2, CH), F32),
            pltpu.VMEM((2, 16, CELLS), F32),
            pltpu.VMEM((2, 16, CELLS), F32),
            pltpu.VMEM((2, 16, CELLS), F32),
            pltpu.VMEM((2, 16, CELLS), F32),
            pltpu.VMEM((16, CELLS), F32),
            pltpu.VMEM((16, CELLS), F32),
            DMA,
            DMA((3,)),
            DMA((3,)),
            DMA((3,)),
            DMA((4,)),
            DMA((4,)),
            DMA,
            DMA,
        ],
        compiler_params=pltpu.CompilerParams(
            collective_id=0, has_side_effects=True, vmem_limit_bytes=44 * 1024 * 1024
        ),
        cost_estimate=pl.CostEstimate(flops=10**10, bytes_accessed=10**7, transcendentals=10**6),
    )(*operands)

    def as_frames(v):
        return jnp.transpose(v.reshape(4, ROWS, FRAMES, COLS), (0, 2, 1, 3))

    next_queue = jnp.where(lax.axis_index("queue") == 0, fresh_noise, as_frames(nxt))
    return as_frames(noise)[None], next_queue[None]


def solution(mesh):
    nq, ns = mesh.shape["queue"], mesh.shape["space"]
    rows = P("queue", None, None, "space", None)
    return jax.shard_map(
        functools.partial(per_device, nq, ns),
        mesh=mesh,
        in_specs=(rows, P(None, None, "space", None)) + (P(),) * 11,
        out_specs=(rows, rows),
        check_vma=False,
    )
```

```python
import functools
import math

import jax
import jax.numpy as jnp
from jax import lax
from jax.experimental import pallas as pl
from jax.experimental.pallas import tpu as pltpu
from jax.sharding import PartitionSpec as P

GROUPS = 32
HEAD_DIM = 64
STEP = 50
NORM_EPS = 1e-05
MESH = pl.DeviceIdType.MESH

CH = 320
FRAMES = 16
COLS = 16
ROWS = 3
CELLS = FRAMES * COLS
PER_GROUP = CH // GROUPS
HEADS = CH // HEAD_DIM
MAIN = 256
REST = CH - MAIN
BF = jnp.bfloat16
F32 = jnp.float32


def dot(a, b):
    return jnp.dot(a, b, preferred_element_type=F32)


def dot_nt(a, b):
    return lax.dot_general(a, b, (((1,), (1,)), ((), ())), preferred_element_type=F32)


def silu_of_half(h):
    return h + h * jnp.tanh(h)


def iota(shape, dim):
    return lax.broadcasted_iota(jnp.int32, shape, dim)


def split3(v):
    hi = v.astype(BF)
    left = v - hi.astype(F32)
    mid = left.astype(BF)
    return hi, mid, (left - mid.astype(F32)).astype(BF)


def stack(parts):
    rows = [p.astype(F32) for p in parts]
    return jnp.concatenate(rows + [jnp.zeros((16 - len(rows), rows[0].shape[1]), F32)], axis=0).astype(BF)


def kernel(
    nq,
    ns,
    ts_hbm,
    map_hbm,
    lat_hbm,
    cin_hbm,
    tw1_hbm,
    tw2_hbm,
    emb_hbm,
    c1_hbm,
    c2_hbm,
    qkv_hbm,
    proj_hbm,
    cout_hbm,
    noise_ref,
    next_ref,
    ts_ref,
    map_ref,
    lat_v,
    cin_v,
    tw1_v,
    tw2_v,
    emb_v,
    c1_v,
    c2_v,
    qkv_v,
    proj_v,
    cout_v,
    load_sem,
    lat_f,
    lat_b,
    shifted,
    cin_f,
    cin_w,
    stream,
    hidden,
    block,
    xm,
    xr,
    kr,
    nr,
    wqkv,
    wproj,
    projected,
    pairs,
    bias,
    cout_f,
    wout,
    attended,
    rows_st,
    stats,
    main_out,
    main_in,
    lat_send,
    lat_recv,
    stat_send,
    stat_recv,
    main_send,
    main_recv,
):
    q = lax.axis_index("queue")
    s = lax.axis_index("space")
    ahead = lax.rem(q + 1, nq)
    behind = lax.rem(q + nq - 1, nq)
    ring = ns // 2
    order = sorted(range(1, ns), key=lambda j: -min(j % ring, ring - j % ring))

    def cells(r, n=1):
        return pl.ds(r * CELLS if isinstance(r, int) else pl.multiple_of(r * CELLS, CELLS), n * CELLS)

    barrier = pltpu.get_barrier_semaphore()

    def greet(j, _):
        peer = lax.rem(s + j, ns)
        pl.semaphore_signal(barrier, inc=1, device_id=(q, peer), device_id_type=MESH)
        return 0

    lax.fori_loop(1, ns, greet, 0)
    pl.semaphore_signal(barrier, inc=1, device_id=(behind, s), device_id_type=MESH)

    loads = [
        pltpu.make_async_copy(src, dst, load_sem.at[i])
        for i, (src, dst) in enumerate(
            (
                (lat_hbm, lat_v),
                (cin_hbm, cin_v),
                (tw1_hbm, tw1_v),
                (tw2_hbm, tw2_v),
                (emb_hbm, emb_v),
                (c1_hbm, c1_v),
                (c2_hbm, c2_v),
                (qkv_hbm, qkv_v),
                (proj_hbm, proj_v),
                (cout_hbm, cout_v),
                (ts_hbm, ts_ref),
                (map_hbm, map_ref),
            )
        )
    ]
    for load in loads:
        load.start()
    load_lat, load_cin, load_tw1, load_tw2, load_emb, load_c1, load_c2, load_qkv, load_proj, load_cout, load_ts, load_map = loads

    load_lat.wait()
    lat_f[12:16, :] = jnp.where(iota((4, CELLS), 0) == 0, 1.0, 0.0)
    for f in range(FRAMES):
        lat_f[0:12, f * COLS : (f + 1) * COLS] = lat_v[pl.ds(f, 12, stride=FRAMES), :]
    own_rows = pl.ds(pl.multiple_of((s + 2) * 16, 16), 16)
    lat_b[own_rows, :] = lat_f[...].astype(BF)
    lat_b[0:32, :] = jnp.zeros((32, CELLS), BF)
    lat_b[(ns + 2) * 16 :, :] = jnp.zeros((32, CELLS), BF)

    pl.semaphore_wait(barrier, ns - 1 + 1)

    lat_sends = {
        j: pltpu.make_async_remote_copy(
            lat_b.at[own_rows],
            lat_b.at[own_rows],
            lat_send,
            lat_recv.at[(1, 2, ns - 2, ns - 1).index(j) if j in (1, 2, ns - 2, ns - 1) else 4],
            device_id=(q, lax.rem(s + j, ns)),
            device_id_type=MESH,
        )
        for j in order
    }
    for j in order:
        lat_sends[j].start()

    load_ts.wait()
    load_map.wait()
    level = ts_ref[map_ref[q]]
    pos = iota((16, CH), 1)
    half = CH // 2
    k = jnp.where(pos < half, pos, pos - half).astype(F32)
    phases = level.astype(F32) * jnp.exp(k * (-math.log(10000.0) / half))
    sinusoid = jnp.where(pos < half, jnp.cos(phases), jnp.sin(phases)).astype(BF)
    load_tw1.wait()
    h = dot(sinusoid, tw1_v[...])
    first_hidden = silu_of_half(0.5 * h).astype(BF)
    load_tw2.wait()
    h = dot(first_hidden, tw2_v[...])
    second = silu_of_half(0.5 * h).astype(BF)
    load_emb.wait()
    bias[...] = dot_nt(second, emb_v[...])[0:1]
    ci = iota((CH, CH), 0) * 6554 >> 16
    cj = iota((CH, CH), 1) * 6554 >> 16
    pairs[...] = jnp.where(ci == cj, 1.0, 0.0).astype(BF)

    load_cin.wait()
    cin_f[36:40, :] = jnp.zeros((4, CH), F32)
    for a in range(3):
        for b in range(3):
            t = a * 3 + b
            cin_f[t * 4 : t * 4 + 4, :] = cin_v[a, b].astype(F32)

    kk = iota((144, 40), 0)
    jj = iota((144, 40), 1)
    tap_b = jnp.where(kk >= 48, 1, 0) + jnp.where(kk >= 96, 1, 0)
    left = kk - 48 * tap_b
    in_block = left & 15
    chan = in_block * 21846 >> 16
    row_of = 3 * (left >> 4) + in_block - 3 * chan

    def place_cin(y, _):
        tap_a = row_of - y
        hit = (tap_a >= 0) & (tap_a < 3) & (in_block < 12) & (jj == (tap_a * 3 + tap_b) * 4 + chan)
        sel = jnp.where(hit, 1.0, 0.0).astype(BF)
        cin_w[y] = dot(sel, cin_f[...].astype(BF)).astype(BF)
        return 0

    lax.fori_loop(0, 7, place_cin, 0)

    xr[:, 192:256] = jnp.zeros((11 * CELLS, 64), BF)

    def shared_passes(which, w):
        for b in range(3):
            for a in range(3):
                kr[which, b, a * REST : (a + 1) * REST, :] = w[a, b, MAIN:CH, 0:MAIN]
            kr[which, b, 3 * REST : 256, :] = jnp.zeros((256 - 3 * REST, MAIN), BF)
        for a in range(3):
            for b in range(3):
                nr[which, a * 256 : (a + 1) * 256, b * REST : (b + 1) * REST] = w[a, b, 0:MAIN, MAIN:CH]
                nr[which, 768 + a * REST : 768 + (a + 1) * REST, b * REST : (b + 1) * REST] = w[
                    a, b, MAIN:CH, MAIN:CH
                ]
        nr[which, :, 3 * REST : 256] = jnp.zeros((1024, 256 - 3 * REST), BF)
        nr[which, 768 + 3 * REST : 1024, :] = jnp.zeros((256 - 3 * REST, 256), BF)

    def shift_blocks(start, n):
        rows = pl.ds(start * 16 if isinstance(start, int) else pl.multiple_of(start * 16, 16), n * 16)
        v = lat_b[rows, :].astype(F32)
        lane = iota((n * 16, CELLS), 1) & (COLS - 1)
        shifted[0, rows, :] = jnp.where(lane == 0, 0.0, pltpu.roll(v, 1, 1)).astype(BF)
        shifted[1, rows, :] = lat_b[rows, :]
        shifted[2, rows, :] = jnp.where(lane == COLS - 1, 0.0, pltpu.roll(v, CELLS - 1, 1)).astype(BF)

    for j in (1, 2, ns - 2, ns - 1):
        lat_sends[j].wait_recv()
    shift_blocks(s, 5)

    def cells_of(slot):
        window = pl.ds(pl.multiple_of(slot * 16, 16), 48)
        return jnp.concatenate([shifted[b, window, :] for b in range(3)], axis=0).astype(F32).T.astype(BF)

    x_in = cells_of(s + 1)
    for y in range(7):
        stream[cells(y + 1), :] = dot(x_in, cin_w[y])
    stream[cells(0), :] = dot(cells_of(s), cin_w[2])
    stream[cells(8), :] = dot(cells_of(s + 2), cin_w[4])

    def row_stats(r, x):
        m = jnp.sum(x, axis=0, keepdims=True) * (1.0 / CELLS)
        rows_st[0, pl.ds(r, 1), :] = m
        rows_st[1, pl.ds(r, 1), :] = jnp.sum((x - m) ** 2, axis=0, keepdims=True)

    def send_stats(phase):
        m = rows_st[0, 0:ROWS, :]
        mean = jnp.sum(m, axis=0, keepdims=True) * (1.0 / ROWS)
        dev = jnp.sum(rows_st[1, 0:ROWS, :] + CELLS * (m - mean) ** 2, axis=0, keepdims=True)
        stats[phase, s] = jnp.concatenate([mean, dev], axis=0)

        for j in order:
            pltpu.make_async_remote_copy(
                stats.at[phase, s],
                stats.at[phase, s],
                stat_send.at[phase],
                stat_recv.at[phase],
                device_id=(q, lax.rem(s + j, ns)),
                device_id_type=MESH,
            ).start()
        near = dot(jnp.broadcast_to(mean, (16, CH)).astype(BF), pairs[...])
        return near[0:1] * (1.0 / PER_GROUP)

    def take_stats(phase, near, shift=0.0):
        pltpu.make_async_copy(
            stats.at[phase, pl.ds(0, ns - 1)], stats.at[phase, pl.ds(0, ns - 1)], stat_recv.at[phase]
        ).wait()
        v = stats[phase]
        d = v - jnp.concatenate([near - shift, jnp.zeros_like(near)], axis=0)
        total = jnp.sum(d, axis=0)
        square = jnp.sum(d * d, axis=0)
        s1 = total[0:1]
        s2 = total[1:2] + (ROWS * CELLS) * square[0:1]
        parts = split3(s1) + split3(s2)
        g = dot(stack(parts), pairs[...])
        off = (g[0:1] + g[1:2] + g[2:3]) * (1.0 / (ns * PER_GROUP))
        spread = (g[3:4] + g[4:5] + g[5:6]) * (1.0 / (ns * PER_GROUP * ROWS * CELLS)) - off * off
        return near + off, lax.rsqrt(jnp.maximum(spread, 0.0) + NORM_EPS)

    def stats_sent(phase):
        pltpu.make_async_copy(
            stats.at[phase, pl.ds(0, ns - 1)], stats.at[phase, pl.ds(0, ns - 1)], stat_send.at[phase]
        ).wait()

    def put_normed(r, y):
        yb = y.astype(BF)
        xm[cells(r), :] = yb[:, 0:MAIN]
        rest = yb[:, MAIN:CH]
        xr[cells(r + 2), 0:REST] = rest
        xr[cells(r + 1), REST : 2 * REST] = rest
        xr[cells(r), 2 * REST : 3 * REST] = rest

    def column(n, width, x):
        return jnp.where((iota((n * CELLS, width), 0) & (COLS - 1)) == x, 0.0, 1.0)

    def conv_rows(which, w, rows):
        n = len(rows)
        size = n * CELLS

        def window(ref, a):
            return jnp.concatenate([ref[cells(y + a), :] for y in rows], axis=0)

        x = jnp.concatenate([window(xm, 0), window(xm, 1), window(xm, 2), window(xr, 2)], axis=1)
        z = [
            dot(
                x,
                jnp.concatenate(
                    [w[0, b, 0:MAIN, 0:MAIN], w[1, b, 0:MAIN, 0:MAIN], w[2, b, 0:MAIN, 0:MAIN], kr[which, b]], axis=0
                ),
            )
            for b in range(3)
        ]
        main = (
            z[1] + column(n, MAIN, 0) * pltpu.roll(z[0], 1, 0) + column(n, MAIN, COLS - 1) * pltpu.roll(z[2], size - 1, 0)
        )
        zr = dot(x, nr[which])
        rest = (
            column(n, REST, 0) * pltpu.roll(zr, 1, 0)[:, 0:REST]
            + zr[:, REST : 2 * REST]
            + column(n, REST, COLS - 1) * pltpu.roll(zr, size - 1, 0)[:, 2 * REST : 3 * REST]
        )
        return main, rest

    load_c1.wait()
    shared_passes(0, c1_v)

    pltpu.make_async_copy(lat_b.at[pl.ds(0, (ns - 5) * 16)], lat_b.at[pl.ds(0, (ns - 5) * 16)], lat_recv.at[4]).wait()
    shift_blocks(1, ns + 2)
    every = jnp.concatenate(
        [jnp.concatenate([shifted[b, n * 16 + 16 : n * 16 + 64, :] for b in range(3)], axis=0) for n in range(ns)], axis=1
    )
    products = jnp.concatenate(split3(dot_nt(every, every)), axis=0)
    first_sum = jnp.zeros((1, CH), F32)
    second_sum = jnp.zeros((1, CH), F32)
    for y in (2, 3, 4):
        w = cin_w[y]
        g = dot(products, w)
        g = g[0:144] + g[144:288] + g[288:432]
        first_sum = first_sum + g[76:77]
        second_sum = second_sum + jnp.sum(w.astype(F32) * g, axis=0, keepdims=True)
    per_cell = 1.0 / (ns * ROWS * CELLS * PER_GROUP)
    g = dot(stack(split3(first_sum) + split3(second_sum)), pairs[...])
    mean = (g[0:1] + g[1:2] + g[2:3]) * per_cell
    spread = (g[3:4] + g[4:5] + g[5:6]) * per_cell - mean * mean
    inv = lax.rsqrt(jnp.maximum(spread, 0.0) + NORM_EPS)
    half_inv = 0.5 * inv

    def normed(r, x, mean, half_inv, row):
        inside = jnp.where((s * ROWS + row >= 0) & (s * ROWS + row < ns * ROWS), half_inv, 0.0)
        put_normed(r, silu_of_half((x - mean) * inside))

    def norm1(r, _):
        normed(r, stream[cells(r), :], mean, half_inv, r - 3)
        return 0

    lax.fori_loop(2, 7, norm1, 0)

    def hidden_rows(rows):
        main, rest = conv_rows(0, c1_v, rows)
        for i, j in enumerate(rows):
            hidden[cells(j), 0:MAIN] = main[i * CELLS : (i + 1) * CELLS]
            hidden[cells(j), MAIN:CH] = rest[i * CELLS : (i + 1) * CELLS]

    hidden_rows((2, 3, 4))
    for i in range(ROWS):
        row_stats(i, hidden[cells(i + 2), :])
    near2 = send_stats(0)

    lax.fori_loop(0, 2, norm1, 0)
    lax.fori_loop(7, 9, norm1, 0)
    hidden_rows((0, 1, 5, 6))
    load_c2.wait()
    shared_passes(1, c2_v)

    mean2, inv2 = take_stats(0, near2, bias[...])
    mean2 = mean2 - bias[...]
    half_inv2 = 0.5 * inv2

    def norm2(r, _):
        normed(r, hidden[cells(r), :], mean2, half_inv2, r - 2)
        return 0

    lax.fori_loop(1, 6, norm2, 0)

    def block_rows(rows):
        main, rest = conv_rows(1, c2_v, rows)
        for i, j in enumerate(rows):
            block[cells(j), 0:MAIN] = stream[cells(j + 2), 0:MAIN] + main[i * CELLS : (i + 1) * CELLS]
            block[cells(j), MAIN:CH] = stream[cells(j + 2), MAIN:CH] + rest[i * CELLS : (i + 1) * CELLS]

    block_rows((1, 2, 3))
    for i in range(ROWS):
        row_stats(i, block[cells(i + 1), :])
    near3 = send_stats(1)

    norm2(0, 0)
    norm2(6, 0)
    block_rows((0, 4))

    load_qkv.wait()
    wqkv[:, 0:CH] = qkv_v[:, 0:CH] * jnp.asarray(HEAD_DIM**-0.5, BF)
    wqkv[:, CH:384] = jnp.zeros((CH, 384 - CH), BF)
    wqkv[:, 384:1024] = qkv_v[:, CH : 3 * CH]
    load_proj.wait()
    wproj[0:64, :] = jnp.zeros((64, CH), BF)
    wproj[64:384, :] = proj_v[...]
    load_cout.wait()
    cout_f[36:40, :] = jnp.zeros((4, CH), F32)
    for a in range(3):
        for b in range(3):
            r = (a * 3 + b) * 4
            cout_f[r : r + 4, :] = cout_v[a, b].astype(F32)
    to = iota((48, 40), 0)
    src = iota((48, 40), 1)
    to_b = to >> 4
    to_row = to & 15
    to_c = to_row * 21846 >> 16
    for i in range(ROWS + 2):
        tap = i - (to_row - 3 * to_c)
        hit = (tap >= 0) & (tap < 3) & (to_row < 12) & (src == (tap * 3 + to_b) * 4 + to_c)
        wout[i] = dot(jnp.where(hit, 1.0, 0.0).astype(BF), cout_f[...].astype(BF)).astype(BF)

    step_of = iota((8, 128), 0) * 128 + iota((8, 128), 1)
    lo, hi = 0.00085**0.5, 0.012**0.5
    beta = (lo + step_of.astype(F32) * ((hi - lo) / 999.0)) ** 2

    def alpha(t):
        v = jnp.where(step_of <= t, 1.0 - beta, 1.0)
        for sh in (64, 32, 16, 8, 4, 2, 1):
            v = v * pltpu.roll(v, sh, 1)
        for sh in (4, 2, 1):
            v = v * pltpu.roll(v, sh, 0)
        return v[0:1, 0:1]

    alpha_now = alpha(level)
    alpha_next = alpha(level - STEP)
    keep = jnp.sqrt(alpha_next / alpha_now)
    gain = jnp.sqrt(1.0 - alpha_next) - keep * jnp.sqrt(1.0 - alpha_now)

    mean3, inv3 = take_stats(1, near3)

    same = ((iota((CELLS, CELLS), 0) ^ iota((CELLS, CELLS), 1)) & (COLS - 1)) == 0
    low_half = iota((CELLS, 128), 1) < HEAD_DIM

    def project(rows):
        projected[rows, :] = dot(((block[rows, :] - mean3) * inv3).astype(BF), wqkv[...]).astype(BF)

    def mix(rows):
        block[rows, :] += dot(attended[rows, :], wproj[...])

    own_cells = cells(1, ROWS)
    project(own_cells)

    def attend_row(i, _):
        row = cells(i)
        ones = jnp.ones((CELLS, 128), BF)

        def head(h):
            qt = projected[row, h // 2 * 128 : h // 2 * 128 + 128]
            if h < HEADS - 1:
                qt = jnp.where(low_half if h % 2 == 0 else jnp.logical_not(low_half), qt, jnp.zeros_like(qt))
            kt = projected[row, 384 + h // 2 * 128 : 512 + h // 2 * 128]
            vt = projected[row, 640 + (h + 1) // 2 * 128 : 768 + (h + 1) // 2 * 128]
            sc = jnp.where(same, dot_nt(qt, kt), -1e30)
            p = jnp.exp(sc - jnp.max(sc, axis=1, keepdims=True)).astype(BF)
            o = dot(p, jnp.concatenate([vt, ones], axis=1))
            return o[:, 0:128] / o[:, 128:256]

        attended[row, 0:128] = jnp.where(low_half, 0.0, head(0)).astype(BF)
        attended[row, 128:256] = jnp.where(low_half, head(1), head(2)).astype(BF)
        attended[row, 256:384] = jnp.where(low_half, head(3), head(4)).astype(BF)
        return 0

    lax.fori_loop(1, ROWS + 1, attend_row, 0)
    mix(own_cells)
    for i in range(ROWS):
        row_stats(i, block[cells(i + 1), :])
    near4 = send_stats(2)

    for i in (0, ROWS + 1):
        project(cells(i))

    def attend_halo(i, _):
        return attend_row(i * (ROWS + 1), 0)

    lax.fori_loop(0, 2, attend_halo, 0)
    for i in (0, ROWS + 1):
        mix(cells(i))

    mean4, inv4 = take_stats(2, near4)
    half_inv4 = 0.5 * inv4

    z = jnp.zeros((48, CELLS), F32)
    for i in range(ROWS + 2):
        row = s * ROWS + i - 1
        inside = jnp.where((row >= 0) & (row < ns * ROWS), half_inv4, 0.0)
        z = z + dot_nt(wout[i], silu_of_half((block[cells(i), :] - mean4) * inside).astype(BF))
    lane = iota((16, CELLS), 1) & (COLS - 1)
    noise = (
        z[16:32]
        + jnp.where(lane == 0, 0.0, pltpu.roll(z[0:16], 1, 1))
        + jnp.where(lane == COLS - 1, 0.0, pltpu.roll(z[32:48], CELLS - 1, 1))
    )
    main_out[...] = keep * lat_f[...] + gain * noise
    main_send_copy = pltpu.make_async_remote_copy(
        main_out, main_in, main_send, main_recv, device_id=(ahead, s), device_id_type=MESH
    )
    main_send_copy.start()

    def put(out, v):
        for f in range(FRAMES):
            out[pl.ds(f, 12, stride=FRAMES), :] = v[0:12, f * COLS : (f + 1) * COLS]

    put(noise_ref, noise)
    main_send_copy.wait_recv()
    put(next_ref, main_in[...])

    pltpu.make_async_copy(lat_b.at[pl.ds(0, (ns - 1) * 16)], lat_b.at[pl.ds(0, (ns - 1) * 16)], lat_send).wait()
    for phase in range(3):
        stats_sent(phase)
    main_send_copy.wait_send()


def per_device(
    nq,
    ns,
    latents,
    fresh_noise,
    timesteps,
    queue_map,
    conv_in_w,
    time_w1,
    time_w2,
    emb_w,
    conv1_w,
    conv2_w,
    qkv_w,
    proj_w,
    conv_out_w,
):
    hbm = pl.BlockSpec(memory_space=pltpu.HBM)
    vmem = pl.BlockSpec(memory_space=pltpu.VMEM)
    latents = jnp.transpose(latents[0], (0, 2, 1, 3)).reshape(4 * ROWS * FRAMES, COLS)
    emb_t = emb_w.T
    out_t = jnp.swapaxes(conv_out_w, 2, 3)
    weights = (conv_in_w, time_w1, time_w2, emb_t, conv1_w, conv2_w, qkv_w, proj_w, out_t)
    DMA = pltpu.SemaphoreType.DMA
    operands = [
        pltpu.with_memory_space_constraint(v, pltpu.HBM) for v in (timesteps, queue_map, latents, *weights)
    ]
    noise, nxt = pl.pallas_call(
        functools.partial(kernel, nq, ns),
        out_shape=(
            jax.ShapeDtypeStruct((4 * ROWS * FRAMES, COLS), F32),
            jax.ShapeDtypeStruct((4 * ROWS * FRAMES, COLS), F32),
        ),
        in_specs=[hbm] * len(operands),
        out_specs=(vmem, vmem),
        scratch_shapes=[pltpu.SMEM(timesteps.shape, jnp.int32), pltpu.SMEM(queue_map.shape, jnp.int32)]
        + [pltpu.VMEM(latents.shape, F32)]
        + [pltpu.VMEM(w.shape, BF) for w in weights]
        + [
            DMA((len(operands),)),
            pltpu.VMEM((16, CELLS), F32),
            pltpu.VMEM(((ns + 4) * 16, CELLS), BF),
            pltpu.VMEM((3, (ns + 4) * 16, CELLS), BF),
            pltpu.VMEM((40, CH), F32),
            pltpu.VMEM((7, 144, CH), BF),
            pltpu.VMEM((9 * CELLS, CH), F32),
            pltpu.VMEM((7 * CELLS, CH), F32),
            pltpu.VMEM((5 * CELLS, CH), F32),
            pltpu.VMEM((9 * CELLS, MAIN), BF),
            pltpu.VMEM((11 * CELLS, 256), BF),
            pltpu.VMEM((2, 3, 256, MAIN), BF),
            pltpu.VMEM((2, 1024, 256), BF),
            pltpu.VMEM((CH, 1024), BF),
            pltpu.VMEM((384, CH), BF),
            pltpu.VMEM(((ROWS + 2) * CELLS, 1024), BF),
            pltpu.VMEM((CH, CH), BF),
            pltpu.VMEM((1, CH), F32),
            pltpu.VMEM((40, CH), F32),
            pltpu.VMEM((5, 48, CH), BF),
            pltpu.VMEM(((ROWS + 2) * CELLS, 384), BF),
            pltpu.VMEM((2, 8, CH), F32),
            pltpu.VMEM((3, ns, 2, CH), F32),
            pltpu.VMEM((16, CELLS), F32),
            pltpu.VMEM((16, CELLS), F32),
            DMA,
            DMA((5,)),
            DMA((3,)),
            DMA((3,)),
            DMA,
            DMA,
        ],
        compiler_params=pltpu.CompilerParams(
            collective_id=0, has_side_effects=True, vmem_limit_bytes=44 * 1024 * 1024
        ),
        cost_estimate=pl.CostEstimate(flops=10**10, bytes_accessed=10**7, transcendentals=10**6),
    )(*operands)

    def as_frames(v):
        return jnp.transpose(v.reshape(4, ROWS, FRAMES, COLS), (0, 2, 1, 3))

    next_queue = jnp.where(lax.axis_index("queue") == 0, fresh_noise, as_frames(nxt))
    return as_frames(noise)[None], next_queue[None]


def solution(mesh):
    nq, ns = mesh.shape["queue"], mesh.shape["space"]
    rows = P("queue", None, None, "space", None)
    return jax.shard_map(
        functools.partial(per_device, nq, ns),
        mesh=mesh,
        in_specs=(rows, P(None, None, "space", None)) + (P(),) * 11,
        out_specs=(rows, rows),
        check_vma=False,
    )
```

```python
import functools
import math

import jax
import jax.numpy as jnp
from jax import lax
from jax.experimental import pallas as pl
from jax.experimental.pallas import tpu as pltpu
from jax.sharding import PartitionSpec as P

GROUPS = 32
HEAD_DIM = 64
STEP = 50
NORM_EPS = 1e-05
MESH = pl.DeviceIdType.MESH

CH = 320
FRAMES = 16
COLS = 16
ROWS = 3
CELLS = FRAMES * COLS
PER_GROUP = CH // GROUPS
HEADS = CH // HEAD_DIM
MAIN = 256
REST = CH - MAIN
BF = jnp.bfloat16
F32 = jnp.float32


def dot(a, b):
    return jnp.dot(a, b, preferred_element_type=F32)


def dot_nt(a, b):
    return lax.dot_general(a, b, (((1,), (1,)), ((), ())), preferred_element_type=F32)


def silu_of_half(h):
    return h + h * jnp.tanh(h)


def iota(shape, dim):
    return lax.broadcasted_iota(jnp.int32, shape, dim)


def split3(v):
    hi = v.astype(BF)
    left = v - hi.astype(F32)
    mid = left.astype(BF)
    return hi, mid, (left - mid.astype(F32)).astype(BF)


def stack(parts):
    rows = [p.astype(F32) for p in parts]
    return jnp.concatenate(rows + [jnp.zeros((16 - len(rows), rows[0].shape[1]), F32)], axis=0).astype(BF)


def kernel(
    nq,
    ns,
    ts_hbm,
    map_hbm,
    lat_hbm,
    cin_hbm,
    tw1_hbm,
    tw2_hbm,
    emb_hbm,
    c1_hbm,
    c2_hbm,
    qkv_hbm,
    proj_hbm,
    cout_hbm,
    noise_ref,
    next_ref,
    ts_ref,
    map_ref,
    lat_v,
    cin_v,
    tw1_v,
    tw2_v,
    emb_v,
    c1_v,
    c2_v,
    qkv_v,
    proj_v,
    cout_v,
    load_sem,
    lat_f,
    lat_b,
    shifted,
    cin_f,
    cin_w,
    stream,
    hidden,
    block,
    xm,
    xr,
    xm2,
    xr2,
    kr,
    nr,
    wqkv,
    wproj,
    projected,
    pairs,
    bias,
    cout_f,
    wout,
    attended,
    rows_st,
    stats,
    main_out,
    main_in,
    lat_send,
    lat_recv,
    stat_send,
    stat_recv,
    main_send,
    main_recv,
):
    q = lax.axis_index("queue")
    s = lax.axis_index("space")
    ahead = lax.rem(q + 1, nq)
    behind = lax.rem(q + nq - 1, nq)
    ring = ns // 2
    order = sorted(range(1, ns), key=lambda j: -min(j % ring, ring - j % ring))

    def cells(r, n=1):
        return pl.ds(r * CELLS if isinstance(r, int) else pl.multiple_of(r * CELLS, CELLS), n * CELLS)

    barrier = pltpu.get_barrier_semaphore()

    for j in order:
        pl.semaphore_signal(barrier, inc=1, device_id=(q, lax.rem(s + j, ns)), device_id_type=MESH)
    pl.semaphore_signal(barrier, inc=1, device_id=(behind, s), device_id_type=MESH)

    loads = [
        pltpu.make_async_copy(src, dst, load_sem.at[i])
        for i, (src, dst) in enumerate(
            (
                (lat_hbm, lat_v),
                (cin_hbm, cin_v),
                (c1_hbm, c1_v),
                (ts_hbm, ts_ref),
                (map_hbm, map_ref),
                (tw1_hbm, tw1_v),
                (tw2_hbm, tw2_v),
                (emb_hbm, emb_v),
                (c2_hbm, c2_v),
                (qkv_hbm, qkv_v),
                (proj_hbm, proj_v),
                (cout_hbm, cout_v),
            )
        )
    ]
    for load in loads:
        load.start()
    load_lat, load_cin, load_c1, load_ts, load_map, load_tw1, load_tw2, load_emb, load_c2, load_qkv, load_proj, load_cout = loads

    load_lat.wait()
    lat_f[12:16, :] = jnp.where(iota((4, CELLS), 0) == 0, 1.0, 0.0)
    for f in range(FRAMES):
        lat_f[0:12, f * COLS : (f + 1) * COLS] = lat_v[pl.ds(f, 12, stride=FRAMES), :]
    own_rows = pl.ds(pl.multiple_of((s + 2) * 16, 16), 16)
    lat_b[own_rows, :] = lat_f[...].astype(BF)
    lat_b[0:32, :] = jnp.zeros((32, CELLS), BF)
    lat_b[(ns + 2) * 16 :, :] = jnp.zeros((32, CELLS), BF)

    pl.semaphore_wait(barrier, ns - 1 + 1)

    lat_sends = {
        j: pltpu.make_async_remote_copy(
            lat_b.at[own_rows],
            lat_b.at[own_rows],
            lat_send,
            lat_recv.at[(1, 2, ns - 2, ns - 1).index(j) if j in (1, 2, ns - 2, ns - 1) else 4],
            device_id=(q, lax.rem(s + j, ns)),
            device_id_type=MESH,
        )
        for j in order
    }
    for j in order:
        lat_sends[j].start()

    ci = iota((CH, CH), 0) * 6554 >> 16
    cj = iota((CH, CH), 1) * 6554 >> 16
    pairs[...] = jnp.where(ci == cj, 1.0, 0.0).astype(BF)

    load_cin.wait()
    cin_f[36:40, :] = jnp.zeros((4, CH), F32)
    for a in range(3):
        for b in range(3):
            t = a * 3 + b
            cin_f[t * 4 : t * 4 + 4, :] = cin_v[a, b].astype(F32)

    kk = iota((144, 40), 0)
    jj = iota((144, 40), 1)
    tap_b = jnp.where(kk >= 48, 1, 0) + jnp.where(kk >= 96, 1, 0)
    left = kk - 48 * tap_b
    in_block = left & 15
    chan = in_block * 21846 >> 16
    row_of = 3 * (left >> 4) + in_block - 3 * chan

    for y in range(7):
        tap_a = row_of - y
        hit = (tap_a >= 0) & (tap_a < 3) & (in_block < 12) & (jj == (tap_a * 3 + tap_b) * 4 + chan)
        sel = jnp.where(hit, 1.0, 0.0).astype(BF)
        cin_w[y] = dot(sel, cin_f[...].astype(BF)).astype(BF)

    xr[:, 192:256] = jnp.zeros((11 * CELLS, 64), BF)
    xr2[:, 192:256] = jnp.zeros((9 * CELLS, 64), BF)

    def shared_passes(which, w):
        for b in range(3):
            for a in range(3):
                kr[which, b, a * REST : (a + 1) * REST, :] = w[a, b, MAIN:CH, 0:MAIN]
            kr[which, b, 3 * REST : 256, :] = jnp.zeros((256 - 3 * REST, MAIN), BF)
        for a in range(3):
            for b in range(3):
                nr[which, a * 256 : (a + 1) * 256, b * REST : (b + 1) * REST] = w[a, b, 0:MAIN, MAIN:CH]
                nr[which, 768 + a * REST : 768 + (a + 1) * REST, b * REST : (b + 1) * REST] = w[
                    a, b, MAIN:CH, MAIN:CH
                ]
        nr[which, :, 3 * REST : 256] = jnp.zeros((1024, 256 - 3 * REST), BF)
        nr[which, 768 + 3 * REST : 1024, :] = jnp.zeros((256 - 3 * REST, 256), BF)

    def shift_blocks(start, n):
        rows = pl.ds(start * 16 if isinstance(start, int) else pl.multiple_of(start * 16, 16), n * 16)
        v = lat_b[rows, :].astype(F32)
        lane = iota((n * 16, CELLS), 1) & (COLS - 1)
        shifted[0, rows, :] = jnp.where(lane == 0, 0.0, pltpu.roll(v, 1, 1)).astype(BF)
        shifted[1, rows, :] = lat_b[rows, :]
        shifted[2, rows, :] = jnp.where(lane == COLS - 1, 0.0, pltpu.roll(v, CELLS - 1, 1)).astype(BF)

    for j in (1, 2, ns - 2, ns - 1):
        lat_sends[j].wait_recv()
    shift_blocks(s, 5)

    def cells_of(slot):
        window = pl.ds(pl.multiple_of(slot * 16, 16), 48)
        return jnp.concatenate([shifted[b, window, :] for b in range(3)], axis=0).astype(F32).T.astype(BF)

    x_in = cells_of(s + 1)
    for y in range(7):
        stream[cells(y + 1), :] = dot(x_in, cin_w[y])
    stream[cells(0), :] = dot(cells_of(s), cin_w[2])
    stream[cells(8), :] = dot(cells_of(s + 2), cin_w[4])

    def row_stats(r, x):
        m = jnp.sum(x, axis=0, keepdims=True) * (1.0 / CELLS)
        rows_st[0, pl.ds(r, 1), :] = m
        rows_st[1, pl.ds(r, 1), :] = jnp.sum((x - m) ** 2, axis=0, keepdims=True)

    def send_stats(phase):
        m = rows_st[0, 0:ROWS, :]
        mean = jnp.sum(m, axis=0, keepdims=True) * (1.0 / ROWS)
        dev = jnp.sum(rows_st[1, 0:ROWS, :] + CELLS * (m - mean) ** 2, axis=0, keepdims=True)
        stats[phase, s] = jnp.concatenate([mean, dev], axis=0)

        for j in order:
            pltpu.make_async_remote_copy(
                stats.at[phase, s],
                stats.at[phase, s],
                stat_send.at[phase],
                stat_recv.at[phase],
                device_id=(q, lax.rem(s + j, ns)),
                device_id_type=MESH,
            ).start()
        near = dot(jnp.broadcast_to(mean, (16, CH)).astype(BF), pairs[...])
        return near[0:1] * (1.0 / PER_GROUP)

    def take_stats(phase, near, shift=0.0):
        pltpu.make_async_copy(
            stats.at[phase, pl.ds(0, ns - 1)], stats.at[phase, pl.ds(0, ns - 1)], stat_recv.at[phase]
        ).wait()
        v = stats[phase]
        d = v - jnp.concatenate([near - shift, jnp.zeros_like(near)], axis=0)
        total = jnp.sum(d, axis=0)
        square = jnp.sum(d * d, axis=0)
        s1 = total[0:1]
        s2 = total[1:2] + (ROWS * CELLS) * square[0:1]
        parts = split3(s1) + split3(s2)
        g = dot(stack(parts), pairs[...])
        off = (g[0:1] + g[1:2] + g[2:3]) * (1.0 / (ns * PER_GROUP))
        spread = (g[3:4] + g[4:5] + g[5:6]) * (1.0 / (ns * PER_GROUP * ROWS * CELLS)) - off * off
        return near + off, lax.rsqrt(jnp.maximum(spread, 0.0) + NORM_EPS)

    def stats_sent(phase):
        pltpu.make_async_copy(
            stats.at[phase, pl.ds(0, ns - 1)], stats.at[phase, pl.ds(0, ns - 1)], stat_send.at[phase]
        ).wait()

    inputs = ((xm, xr), (xm2, xr2))

    def put_normed(which, r, y):
        yb = y.astype(BF)
        alone, shared = inputs[which]
        alone[cells(r), :] = yb[:, 0:MAIN]
        rest = yb[:, MAIN:CH]
        shared[cells(r + 2), 0:REST] = rest
        shared[cells(r + 1), REST : 2 * REST] = rest
        shared[cells(r), 2 * REST : 3 * REST] = rest

    def column(n, width, x):
        return jnp.where((iota((n * CELLS, width), 0) & (COLS - 1)) == x, 0.0, 1.0)

    def conv_rows(which, w, rows):
        alone, shared = inputs[which]
        n = len(rows)
        size = n * CELLS

        def window(ref, a):
            return jnp.concatenate([ref[cells(y + a), :] for y in rows], axis=0)

        x = jnp.concatenate([window(alone, 0), window(alone, 1), window(alone, 2), window(shared, 2)], axis=1)
        z = [
            dot(
                x,
                jnp.concatenate(
                    [w[0, b, 0:MAIN, 0:MAIN], w[1, b, 0:MAIN, 0:MAIN], w[2, b, 0:MAIN, 0:MAIN], kr[which, b]], axis=0
                ),
            )
            for b in range(3)
        ]
        main = (
            z[1] + column(n, MAIN, 0) * pltpu.roll(z[0], 1, 0) + column(n, MAIN, COLS - 1) * pltpu.roll(z[2], size - 1, 0)
        )
        zr = dot(x, nr[which])
        rest = (
            column(n, REST, 0) * pltpu.roll(zr, 1, 0)[:, 0:REST]
            + zr[:, REST : 2 * REST]
            + column(n, REST, COLS - 1) * pltpu.roll(zr, size - 1, 0)[:, 2 * REST : 3 * REST]
        )
        return main, rest

    load_c1.wait()
    shared_passes(0, c1_v)

    pltpu.make_async_copy(lat_b.at[pl.ds(0, (ns - 5) * 16)], lat_b.at[pl.ds(0, (ns - 5) * 16)], lat_recv.at[4]).wait()
    shift_blocks(1, ns + 2)
    every = jnp.concatenate(
        [jnp.concatenate([shifted[b, n * 16 + 16 : n * 16 + 64, :] for b in range(3)], axis=0) for n in range(ns)], axis=1
    )
    products = jnp.concatenate(split3(dot_nt(every, every)), axis=0)
    first_sum = jnp.zeros((1, CH), F32)
    second_sum = jnp.zeros((1, CH), F32)
    for y in (2, 3, 4):
        w = cin_w[y]
        g = dot(products, w)
        g = g[0:144] + g[144:288] + g[288:432]
        first_sum = first_sum + g[76:77]
        second_sum = second_sum + jnp.sum(w.astype(F32) * g, axis=0, keepdims=True)
    per_cell = 1.0 / (ns * ROWS * CELLS * PER_GROUP)
    g = dot(stack(split3(first_sum) + split3(second_sum)), pairs[...])
    mean = (g[0:1] + g[1:2] + g[2:3]) * per_cell
    spread = (g[3:4] + g[4:5] + g[5:6]) * per_cell - mean * mean
    inv = lax.rsqrt(jnp.maximum(spread, 0.0) + NORM_EPS)
    half_inv = 0.5 * inv

    def normed(which, r, x, mean, half_inv, row):
        inside = jnp.where((s * ROWS + row >= 0) & (s * ROWS + row < ns * ROWS), half_inv, 0.0)
        put_normed(which, r, silu_of_half((x - mean) * inside))

    def norm1(r):
        normed(0, r, stream[cells(r), :], mean, half_inv, r - 3)

    for r in range(2, 7):
        norm1(r)

    def hidden_rows(rows):
        main, rest = conv_rows(0, c1_v, rows)
        for i, j in enumerate(rows):
            hidden[cells(j), 0:MAIN] = main[i * CELLS : (i + 1) * CELLS]
            hidden[cells(j), MAIN:CH] = rest[i * CELLS : (i + 1) * CELLS]

    hidden_rows((2, 3, 4))
    for i in range(ROWS):
        row_stats(i, hidden[cells(i + 2), :])
    near2 = send_stats(0)

    norm1(1)
    norm1(7)
    hidden_rows((1, 5))

    load_ts.wait()
    load_map.wait()
    level = ts_ref[map_ref[q]]
    pos = iota((16, CH), 1)
    half = CH // 2
    k = jnp.where(pos < half, pos, pos - half).astype(F32)
    phases = level.astype(F32) * jnp.exp(k * (-math.log(10000.0) / half))
    sinusoid = jnp.where(pos < half, jnp.cos(phases), jnp.sin(phases)).astype(BF)
    load_tw1.wait()
    h = dot(sinusoid, tw1_v[...])
    first_hidden = silu_of_half(0.5 * h).astype(BF)
    load_tw2.wait()
    h = dot(first_hidden, tw2_v[...])
    second = silu_of_half(0.5 * h).astype(BF)
    load_emb.wait()
    bias[...] = dot_nt(second, emb_v[...])[0:1]
    load_c2.wait()
    shared_passes(1, c2_v)

    mean2, inv2 = take_stats(0, near2, bias[...])
    mean2 = mean2 - bias[...]
    half_inv2 = 0.5 * inv2

    def norm2(r):
        normed(1, r, hidden[cells(r), :], mean2, half_inv2, r - 2)

    for r in range(1, 6):
        norm2(r)

    def block_rows(rows):
        main, rest = conv_rows(1, c2_v, rows)
        for i, j in enumerate(rows):
            block[cells(j), 0:MAIN] = stream[cells(j + 2), 0:MAIN] + main[i * CELLS : (i + 1) * CELLS]
            block[cells(j), MAIN:CH] = stream[cells(j + 2), MAIN:CH] + rest[i * CELLS : (i + 1) * CELLS]

    block_rows((1, 2, 3))
    for i in range(ROWS):
        row_stats(i, block[cells(i + 1), :])
    near3 = send_stats(1)

    norm1(0)
    norm1(8)
    hidden_rows((0, 6))
    norm2(0)
    norm2(6)
    block_rows((0, 4))

    load_qkv.wait()
    wqkv[:, 0:CH] = qkv_v[:, 0:CH] * jnp.asarray(HEAD_DIM**-0.5, BF)
    wqkv[:, CH:384] = jnp.zeros((CH, 384 - CH), BF)
    wqkv[:, 384:1024] = qkv_v[:, CH : 3 * CH]
    load_proj.wait()
    wproj[0:64, :] = jnp.zeros((64, CH), BF)
    wproj[64:384, :] = proj_v[...]
    load_cout.wait()
    cout_f[36:40, :] = jnp.zeros((4, CH), F32)
    for a in range(3):
        for b in range(3):
            r = (a * 3 + b) * 4
            cout_f[r : r + 4, :] = cout_v[a, b].astype(F32)
    to = iota((48, 40), 0)
    src = iota((48, 40), 1)
    to_b = to >> 4
    to_row = to & 15
    to_c = to_row * 21846 >> 16
    for i in range(ROWS + 2):
        tap = i - (to_row - 3 * to_c)
        hit = (tap >= 0) & (tap < 3) & (to_row < 12) & (src == (tap * 3 + to_b) * 4 + to_c)
        wout[i] = dot(jnp.where(hit, 1.0, 0.0).astype(BF), cout_f[...].astype(BF)).astype(BF)

    step_of = iota((8, 128), 0) * 128 + iota((8, 128), 1)
    lo, hi = 0.00085**0.5, 0.012**0.5
    beta = (lo + step_of.astype(F32) * ((hi - lo) / 999.0)) ** 2

    def alpha(t):
        v = jnp.where(step_of <= t, 1.0 - beta, 1.0)
        for sh in (64, 32, 16, 8, 4, 2, 1):
            v = v * pltpu.roll(v, sh, 1)
        for sh in (4, 2, 1):
            v = v * pltpu.roll(v, sh, 0)
        return v[0:1, 0:1]

    alpha_now = alpha(level)
    alpha_next = alpha(level - STEP)
    keep = jnp.sqrt(alpha_next / alpha_now)
    gain = jnp.sqrt(1.0 - alpha_next) - keep * jnp.sqrt(1.0 - alpha_now)

    mean3, inv3 = take_stats(1, near3)

    same = ((iota((CELLS, CELLS), 0) ^ iota((CELLS, CELLS), 1)) & (COLS - 1)) == 0
    low_half = iota((CELLS, 128), 1) < HEAD_DIM

    def project(rows):
        projected[rows, :] = dot(((block[rows, :] - mean3) * inv3).astype(BF), wqkv[...]).astype(BF)

    def mix(rows):
        block[rows, :] += dot(attended[rows, :], wproj[...])

    own_cells = cells(1, ROWS)
    project(own_cells)

    def attend_row(i):
        row = cells(i)
        ones = jnp.ones((CELLS, 128), BF)

        def head(h):
            qt = projected[row, h // 2 * 128 : h // 2 * 128 + 128]
            if h < HEADS - 1:
                qt = jnp.where(low_half if h % 2 == 0 else jnp.logical_not(low_half), qt, jnp.zeros_like(qt))
            kt = projected[row, 384 + h // 2 * 128 : 512 + h // 2 * 128]
            vt = projected[row, 640 + (h + 1) // 2 * 128 : 768 + (h + 1) // 2 * 128]
            sc = jnp.where(same, dot_nt(qt, kt), -1e30)
            p = jnp.exp(sc - jnp.max(sc, axis=1, keepdims=True)).astype(BF)
            o = dot(p, jnp.concatenate([vt, ones], axis=1))
            return o[:, 0:128] / o[:, 128:256]

        attended[row, 0:128] = jnp.where(low_half, 0.0, head(0)).astype(BF)
        attended[row, 128:256] = jnp.where(low_half, head(1), head(2)).astype(BF)
        attended[row, 256:384] = jnp.where(low_half, head(3), head(4)).astype(BF)

    for i in range(1, ROWS + 1):
        attend_row(i)
    mix(own_cells)
    for i in range(ROWS):
        row_stats(i, block[cells(i + 1), :])
    near4 = send_stats(2)

    for i in (0, ROWS + 1):
        project(cells(i))

    for i in (0, ROWS + 1):
        attend_row(i)
    for i in (0, ROWS + 1):
        mix(cells(i))

    mean4, inv4 = take_stats(2, near4)
    half_inv4 = 0.5 * inv4

    z = jnp.zeros((48, CELLS), F32)
    for i in range(ROWS + 2):
        row = s * ROWS + i - 1
        inside = jnp.where((row >= 0) & (row < ns * ROWS), half_inv4, 0.0)
        z = z + dot_nt(wout[i], silu_of_half((block[cells(i), :] - mean4) * inside).astype(BF))
    lane = iota((16, CELLS), 1) & (COLS - 1)
    noise = (
        z[16:32]
        + jnp.where(lane == 0, 0.0, pltpu.roll(z[0:16], 1, 1))
        + jnp.where(lane == COLS - 1, 0.0, pltpu.roll(z[32:48], CELLS - 1, 1))
    )
    main_out[...] = keep * lat_f[...] + gain * noise
    main_send_copy = pltpu.make_async_remote_copy(
        main_out, main_in, main_send, main_recv, device_id=(ahead, s), device_id_type=MESH
    )
    main_send_copy.start()

    def put(out, v):
        for f in range(FRAMES):
            out[pl.ds(f, 12, stride=FRAMES), :] = v[0:12, f * COLS : (f + 1) * COLS]

    put(noise_ref, noise)
    main_send_copy.wait_recv()
    put(next_ref, main_in[...])

    pltpu.make_async_copy(lat_b.at[pl.ds(0, (ns - 1) * 16)], lat_b.at[pl.ds(0, (ns - 1) * 16)], lat_send).wait()
    for phase in range(3):
        stats_sent(phase)
    main_send_copy.wait_send()


def per_device(
    nq,
    ns,
    latents,
    fresh_noise,
    timesteps,
    queue_map,
    conv_in_w,
    time_w1,
    time_w2,
    emb_w,
    conv1_w,
    conv2_w,
    qkv_w,
    proj_w,
    conv_out_w,
):
    hbm = pl.BlockSpec(memory_space=pltpu.HBM)
    vmem = pl.BlockSpec(memory_space=pltpu.VMEM)
    latents = jnp.transpose(latents[0], (0, 2, 1, 3)).reshape(4 * ROWS * FRAMES, COLS)
    emb_t = emb_w.T
    out_t = jnp.swapaxes(conv_out_w, 2, 3)
    weights = (conv_in_w, time_w1, time_w2, emb_t, conv1_w, conv2_w, qkv_w, proj_w, out_t)
    DMA = pltpu.SemaphoreType.DMA
    operands = [
        pltpu.with_memory_space_constraint(v, pltpu.HBM) for v in (timesteps, queue_map, latents, *weights)
    ]
    noise, nxt = pl.pallas_call(
        functools.partial(kernel, nq, ns),
        out_shape=(
            jax.ShapeDtypeStruct((4 * ROWS * FRAMES, COLS), F32),
            jax.ShapeDtypeStruct((4 * ROWS * FRAMES, COLS), F32),
        ),
        in_specs=[hbm] * len(operands),
        out_specs=(vmem, vmem),
        scratch_shapes=[pltpu.SMEM(timesteps.shape, jnp.int32), pltpu.SMEM(queue_map.shape, jnp.int32)]
        + [pltpu.VMEM(latents.shape, F32)]
        + [pltpu.VMEM(w.shape, BF) for w in weights]
        + [
            DMA((len(operands),)),
            pltpu.VMEM((16, CELLS), F32),
            pltpu.VMEM(((ns + 4) * 16, CELLS), BF),
            pltpu.VMEM((3, (ns + 4) * 16, CELLS), BF),
            pltpu.VMEM((40, CH), F32),
            pltpu.VMEM((7, 144, CH), BF),
            pltpu.VMEM((9 * CELLS, CH), F32),
            pltpu.VMEM((7 * CELLS, CH), F32),
            pltpu.VMEM((5 * CELLS, CH), F32),
            pltpu.VMEM((9 * CELLS, MAIN), BF),
            pltpu.VMEM((11 * CELLS, 256), BF),
            pltpu.VMEM((7 * CELLS, MAIN), BF),
            pltpu.VMEM((9 * CELLS, 256), BF),
            pltpu.VMEM((2, 3, 256, MAIN), BF),
            pltpu.VMEM((2, 1024, 256), BF),
            pltpu.VMEM((CH, 1024), BF),
            pltpu.VMEM((384, CH), BF),
            pltpu.VMEM(((ROWS + 2) * CELLS, 1024), BF),
            pltpu.VMEM((CH, CH), BF),
            pltpu.VMEM((1, CH), F32),
            pltpu.VMEM((40, CH), F32),
            pltpu.VMEM((5, 48, CH), BF),
            pltpu.VMEM(((ROWS + 2) * CELLS, 384), BF),
            pltpu.VMEM((2, 8, CH), F32),
            pltpu.VMEM((3, ns, 2, CH), F32),
            pltpu.VMEM((16, CELLS), F32),
            pltpu.VMEM((16, CELLS), F32),
            DMA,
            DMA((5,)),
            DMA((3,)),
            DMA((3,)),
            DMA,
            DMA,
        ],
        compiler_params=pltpu.CompilerParams(
            collective_id=0, has_side_effects=True, vmem_limit_bytes=44 * 1024 * 1024
        ),
        cost_estimate=pl.CostEstimate(flops=10**10, bytes_accessed=10**7, transcendentals=10**6),
    )(*operands)

    def as_frames(v):
        return jnp.transpose(v.reshape(4, ROWS, FRAMES, COLS), (0, 2, 1, 3))

    next_queue = jnp.where(lax.axis_index("queue") == 0, fresh_noise, as_frames(nxt))
    return as_frames(noise)[None], next_queue[None]


def solution(mesh):
    nq, ns = mesh.shape["queue"], mesh.shape["space"]
    rows = P("queue", None, None, "space", None)
    return jax.shard_map(
        functools.partial(per_device, nq, ns),
        mesh=mesh,
        in_specs=(rows, P(None, None, "space", None)) + (P(),) * 11,
        out_specs=(rows, rows),
        check_vma=False,
    )
```

```python
import functools
import math

import jax
import jax.numpy as jnp
from jax import lax
from jax.experimental import pallas as pl
from jax.experimental.pallas import tpu as pltpu
from jax.sharding import PartitionSpec as P

GROUPS = 32
HEAD_DIM = 64
STEP = 50
NORM_EPS = 1e-05
MESH = pl.DeviceIdType.MESH

CH = 320
FRAMES = 16
COLS = 16
ROWS = 3
CELLS = FRAMES * COLS
PER_GROUP = CH // GROUPS
HEADS = CH // HEAD_DIM
MAIN = 256
REST = CH - MAIN
BF = jnp.bfloat16
F32 = jnp.float32


def dot(a, b):
    return jnp.dot(a, b, preferred_element_type=F32)


def dot_nt(a, b):
    return lax.dot_general(a, b, (((1,), (1,)), ((), ())), preferred_element_type=F32)


def silu_of_half(h):
    return h + h * jnp.tanh(h)


def iota(shape, dim):
    return lax.broadcasted_iota(jnp.int32, shape, dim)


def split3(v):
    hi = v.astype(BF)
    left = v - hi.astype(F32)
    mid = left.astype(BF)
    return hi, mid, (left - mid.astype(F32)).astype(BF)


def stack(parts):
    rows = [p.astype(F32) for p in parts]
    return jnp.concatenate(rows + [jnp.zeros((16 - len(rows), rows[0].shape[1]), F32)], axis=0).astype(BF)


def kernel(
    nq,
    ns,
    ts_hbm,
    map_hbm,
    lat_hbm,
    cin_hbm,
    tw1_hbm,
    tw2_hbm,
    emb_hbm,
    c1_hbm,
    c2_hbm,
    qkv_hbm,
    proj_hbm,
    cout_hbm,
    noise_ref,
    next_ref,
    ts_ref,
    map_ref,
    lat_v,
    cin_v,
    tw1_v,
    tw2_v,
    emb_v,
    c1_v,
    c2_v,
    qkv_v,
    proj_v,
    cout_v,
    load_sem,
    lat_f,
    lat_b,
    shifted,
    cin_f,
    cin_w,
    stream,
    hidden,
    block,
    xm,
    xr,
    xm2,
    xr2,
    kr,
    nr,
    wqkv,
    wproj,
    projected,
    pairs,
    bias,
    cout_f,
    wout,
    attended,
    rows_st,
    stats,
    main_out,
    main_in,
    lat_send,
    lat_recv,
    stat_send,
    stat_recv,
    main_send,
    main_recv,
):
    q = lax.axis_index("queue")
    s = lax.axis_index("space")
    ahead = lax.rem(q + 1, nq)
    behind = lax.rem(q + nq - 1, nq)
    ring = ns // 2
    order = sorted(range(1, ns), key=lambda j: -min(j % ring, ring - j % ring))

    def cells(r, n=1):
        return pl.ds(r * CELLS if isinstance(r, int) else pl.multiple_of(r * CELLS, CELLS), n * CELLS)

    barrier = pltpu.get_barrier_semaphore()

    for j in order:
        pl.semaphore_signal(barrier, inc=1, device_id=(q, lax.rem(s + j, ns)), device_id_type=MESH)
    pl.semaphore_signal(barrier, inc=1, device_id=(behind, s), device_id_type=MESH)

    loads = [
        pltpu.make_async_copy(src, dst, load_sem.at[i])
        for i, (src, dst) in enumerate(
            (
                (lat_hbm, lat_v),
                (cin_hbm, cin_v),
                (c1_hbm, c1_v),
                (ts_hbm, ts_ref),
                (map_hbm, map_ref),
                (tw1_hbm, tw1_v),
                (tw2_hbm, tw2_v),
                (emb_hbm, emb_v),
                (c2_hbm, c2_v),
                (qkv_hbm, qkv_v),
                (proj_hbm, proj_v),
                (cout_hbm, cout_v),
            )
        )
    ]
    for load in loads:
        load.start()
    load_lat, load_cin, load_c1, load_ts, load_map, load_tw1, load_tw2, load_emb, load_c2, load_qkv, load_proj, load_cout = loads

    load_lat.wait()
    lat_f[12:16, :] = jnp.where(iota((4, CELLS), 0) == 0, 1.0, 0.0)
    for f in range(FRAMES):
        lat_f[0:12, f * COLS : (f + 1) * COLS] = lat_v[pl.ds(f, 12, stride=FRAMES), :]
    own_rows = pl.ds(pl.multiple_of((s + 2) * 16, 16), 16)
    lat_b[own_rows, :] = lat_f[...].astype(BF)
    lat_b[0:32, :] = jnp.zeros((32, CELLS), BF)
    lat_b[(ns + 2) * 16 :, :] = jnp.zeros((32, CELLS), BF)

    pl.semaphore_wait(barrier, ns - 1 + 1)

    lat_sends = {
        j: pltpu.make_async_remote_copy(
            lat_b.at[own_rows],
            lat_b.at[own_rows],
            lat_send,
            lat_recv.at[(1, 2, ns - 2, ns - 1).index(j) if j in (1, 2, ns - 2, ns - 1) else 4],
            device_id=(q, lax.rem(s + j, ns)),
            device_id_type=MESH,
        )
        for j in order
    }
    for j in order:
        lat_sends[j].start()

    ci = iota((CH, CH), 0) * 6554 >> 16
    cj = iota((CH, CH), 1) * 6554 >> 16
    pairs[...] = jnp.where(ci == cj, 1.0, 0.0).astype(BF)

    load_cin.wait()
    cin_f[36:40, :] = jnp.zeros((4, CH), F32)
    for a in range(3):
        for b in range(3):
            t = a * 3 + b
            cin_f[t * 4 : t * 4 + 4, :] = cin_v[a, b].astype(F32)

    kk = iota((144, 40), 0)
    jj = iota((144, 40), 1)
    tap_b = jnp.where(kk >= 48, 1, 0) + jnp.where(kk >= 96, 1, 0)
    left = kk - 48 * tap_b
    in_block = left & 15
    chan = in_block * 21846 >> 16
    row_of = 3 * (left >> 4) + in_block - 3 * chan

    for y in range(7):
        tap_a = row_of - y
        hit = (tap_a >= 0) & (tap_a < 3) & (in_block < 12) & (jj == (tap_a * 3 + tap_b) * 4 + chan)
        sel = jnp.where(hit, 1.0, 0.0).astype(BF)
        cin_w[y] = dot(sel, cin_f[...].astype(BF)).astype(BF)

    xr[:, 192:256] = jnp.zeros((11 * CELLS, 64), BF)
    xr2[:, 192:256] = jnp.zeros((9 * CELLS, 64), BF)

    def shared_passes(which, w):
        for b in range(3):
            for a in range(3):
                kr[which, b, a * REST : (a + 1) * REST, :] = w[a, b, MAIN:CH, 0:MAIN]
            kr[which, b, 3 * REST : 256, :] = jnp.zeros((256 - 3 * REST, MAIN), BF)
        for a in range(3):
            for b in range(3):
                nr[which, a * 256 : (a + 1) * 256, b * REST : (b + 1) * REST] = w[a, b, 0:MAIN, MAIN:CH]
                nr[which, 768 + a * REST : 768 + (a + 1) * REST, b * REST : (b + 1) * REST] = w[
                    a, b, MAIN:CH, MAIN:CH
                ]
        nr[which, :, 3 * REST : 256] = jnp.zeros((1024, 256 - 3 * REST), BF)
        nr[which, 768 + 3 * REST : 1024, :] = jnp.zeros((256 - 3 * REST, 256), BF)

    def shift_blocks(start, n):
        rows = pl.ds(start * 16 if isinstance(start, int) else pl.multiple_of(start * 16, 16), n * 16)
        v = lat_b[rows, :].astype(F32)
        lane = iota((n * 16, CELLS), 1) & (COLS - 1)
        shifted[0, rows, :] = jnp.where(lane == 0, 0.0, pltpu.roll(v, 1, 1)).astype(BF)
        shifted[1, rows, :] = lat_b[rows, :]
        shifted[2, rows, :] = jnp.where(lane == COLS - 1, 0.0, pltpu.roll(v, CELLS - 1, 1)).astype(BF)

    load_c1.wait()
    shared_passes(0, c1_v)
    for j in (1, 2, ns - 2, ns - 1):
        lat_sends[j].wait_recv()
    shift_blocks(s, 5)

    def cells_of(slot):
        window = pl.ds(pl.multiple_of(slot * 16, 16), 48)
        return jnp.concatenate([shifted[b, window, :] for b in range(3)], axis=0).astype(F32).T.astype(BF)

    x_in = cells_of(s + 1)
    for y in range(1, 6):
        stream[cells(y + 1), :] = dot(x_in, cin_w[y])

    def row_stats(r, x):
        m = jnp.sum(x, axis=0, keepdims=True) * (1.0 / CELLS)
        rows_st[0, pl.ds(r, 1), :] = m
        rows_st[1, pl.ds(r, 1), :] = jnp.sum((x - m) ** 2, axis=0, keepdims=True)

    def send_stats(phase):
        m = rows_st[0, 0:ROWS, :]
        mean = jnp.sum(m, axis=0, keepdims=True) * (1.0 / ROWS)
        dev = jnp.sum(rows_st[1, 0:ROWS, :] + CELLS * (m - mean) ** 2, axis=0, keepdims=True)
        stats[phase, s] = jnp.concatenate([mean, dev], axis=0)

        for j in order:
            pltpu.make_async_remote_copy(
                stats.at[phase, s],
                stats.at[phase, s],
                stat_send.at[phase],
                stat_recv.at[phase],
                device_id=(q, lax.rem(s + j, ns)),
                device_id_type=MESH,
            ).start()
        near = dot(jnp.broadcast_to(mean, (16, CH)).astype(BF), pairs[...])
        return near[0:1] * (1.0 / PER_GROUP)

    def take_stats(phase, near, shift=0.0):
        pltpu.make_async_copy(
            stats.at[phase, pl.ds(0, ns - 1)], stats.at[phase, pl.ds(0, ns - 1)], stat_recv.at[phase]
        ).wait()
        v = stats[phase]
        d = v - jnp.concatenate([near - shift, jnp.zeros_like(near)], axis=0)
        total = jnp.sum(d, axis=0)
        square = jnp.sum(d * d, axis=0)
        s1 = total[0:1]
        s2 = total[1:2] + (ROWS * CELLS) * square[0:1]
        parts = split3(s1) + split3(s2)
        g = dot(stack(parts), pairs[...])
        off = (g[0:1] + g[1:2] + g[2:3]) * (1.0 / (ns * PER_GROUP))
        spread = (g[3:4] + g[4:5] + g[5:6]) * (1.0 / (ns * PER_GROUP * ROWS * CELLS)) - off * off
        return near + off, lax.rsqrt(jnp.maximum(spread, 0.0) + NORM_EPS)

    def stats_sent(phase):
        pltpu.make_async_copy(
            stats.at[phase, pl.ds(0, ns - 1)], stats.at[phase, pl.ds(0, ns - 1)], stat_send.at[phase]
        ).wait()

    inputs = ((xm, xr), (xm2, xr2))

    def put_normed(which, r, y):
        yb = y.astype(BF)
        alone, shared = inputs[which]
        alone[cells(r), :] = yb[:, 0:MAIN]
        rest = yb[:, MAIN:CH]
        shared[cells(r + 2), 0:REST] = rest
        shared[cells(r + 1), REST : 2 * REST] = rest
        shared[cells(r), 2 * REST : 3 * REST] = rest

    def column(n, width, x):
        return jnp.where((iota((n * CELLS, width), 0) & (COLS - 1)) == x, 0.0, 1.0)

    def conv_rows(which, w, rows):
        alone, shared = inputs[which]
        n = len(rows)
        size = n * CELLS

        def window(ref, a):
            return jnp.concatenate([ref[cells(y + a), :] for y in rows], axis=0)

        x = jnp.concatenate([window(alone, 0), window(alone, 1), window(alone, 2), window(shared, 2)], axis=1)
        z = [
            dot(
                x,
                jnp.concatenate(
                    [w[0, b, 0:MAIN, 0:MAIN], w[1, b, 0:MAIN, 0:MAIN], w[2, b, 0:MAIN, 0:MAIN], kr[which, b]], axis=0
                ),
            )
            for b in range(3)
        ]
        main = (
            z[1] + column(n, MAIN, 0) * pltpu.roll(z[0], 1, 0) + column(n, MAIN, COLS - 1) * pltpu.roll(z[2], size - 1, 0)
        )
        zr = dot(x, nr[which])
        rest = (
            column(n, REST, 0) * pltpu.roll(zr, 1, 0)[:, 0:REST]
            + zr[:, REST : 2 * REST]
            + column(n, REST, COLS - 1) * pltpu.roll(zr, size - 1, 0)[:, 2 * REST : 3 * REST]
        )
        return main, rest


    pltpu.make_async_copy(lat_b.at[pl.ds(0, (ns - 5) * 16)], lat_b.at[pl.ds(0, (ns - 5) * 16)], lat_recv.at[4]).wait()
    shift_blocks(1, ns + 2)
    every = jnp.concatenate(
        [jnp.concatenate([shifted[b, n * 16 + 16 : n * 16 + 64, :] for b in range(3)], axis=0) for n in range(ns)], axis=1
    )
    products = jnp.concatenate(split3(dot_nt(every, every)), axis=0)
    first_sum = jnp.zeros((1, CH), F32)
    second_sum = jnp.zeros((1, CH), F32)
    for y in (2, 3, 4):
        w = cin_w[y]
        g = dot(products, w)
        g = g[0:144] + g[144:288] + g[288:432]
        first_sum = first_sum + g[76:77]
        second_sum = second_sum + jnp.sum(w.astype(F32) * g, axis=0, keepdims=True)
    per_cell = 1.0 / (ns * ROWS * CELLS * PER_GROUP)
    g = dot(stack(split3(first_sum) + split3(second_sum)), pairs[...])
    mean = (g[0:1] + g[1:2] + g[2:3]) * per_cell
    spread = (g[3:4] + g[4:5] + g[5:6]) * per_cell - mean * mean
    inv = lax.rsqrt(jnp.maximum(spread, 0.0) + NORM_EPS)
    half_inv = 0.5 * inv

    def normed(which, r, x, mean, half_inv, row):
        inside = jnp.where((s * ROWS + row >= 0) & (s * ROWS + row < ns * ROWS), half_inv, 0.0)
        put_normed(which, r, silu_of_half((x - mean) * inside))

    def norm1(r):
        normed(0, r, stream[cells(r), :], mean, half_inv, r - 3)

    for r in range(2, 7):
        norm1(r)

    def hidden_rows(rows):
        main, rest = conv_rows(0, c1_v, rows)
        for i, j in enumerate(rows):
            hidden[cells(j), 0:MAIN] = main[i * CELLS : (i + 1) * CELLS]
            hidden[cells(j), MAIN:CH] = rest[i * CELLS : (i + 1) * CELLS]

    hidden_rows((2, 3, 4))
    for i in range(ROWS):
        row_stats(i, hidden[cells(i + 2), :])
    near2 = send_stats(0)

    x_in = cells_of(s + 1)
    stream[cells(1), :] = dot(x_in, cin_w[0])
    stream[cells(7), :] = dot(x_in, cin_w[6])
    norm1(1)
    norm1(7)
    hidden_rows((1, 5))

    load_ts.wait()
    load_map.wait()
    level = ts_ref[map_ref[q]]
    pos = iota((16, CH), 1)
    half = CH // 2
    k = jnp.where(pos < half, pos, pos - half).astype(F32)
    phases = level.astype(F32) * jnp.exp(k * (-math.log(10000.0) / half))
    sinusoid = jnp.where(pos < half, jnp.cos(phases), jnp.sin(phases)).astype(BF)
    load_tw1.wait()
    h = dot(sinusoid, tw1_v[...])
    first_hidden = silu_of_half(0.5 * h).astype(BF)
    load_tw2.wait()
    h = dot(first_hidden, tw2_v[...])
    second = silu_of_half(0.5 * h).astype(BF)
    load_emb.wait()
    bias[...] = dot_nt(second, emb_v[...])[0:1]
    load_c2.wait()
    shared_passes(1, c2_v)
    load_qkv.wait()
    wqkv[:, 0:CH] = qkv_v[:, 0:CH] * jnp.asarray(HEAD_DIM**-0.5, BF)
    wqkv[:, CH:384] = jnp.zeros((CH, 384 - CH), BF)
    wqkv[:, 384:1024] = qkv_v[:, CH : 3 * CH]
    load_proj.wait()
    wproj[0:64, :] = jnp.zeros((64, CH), BF)
    wproj[64:384, :] = proj_v[...]

    mean2, inv2 = take_stats(0, near2, bias[...])
    mean2 = mean2 - bias[...]
    half_inv2 = 0.5 * inv2

    def norm2(r):
        normed(1, r, hidden[cells(r), :], mean2, half_inv2, r - 2)

    for r in range(1, 6):
        norm2(r)

    def block_rows(rows):
        main, rest = conv_rows(1, c2_v, rows)
        for i, j in enumerate(rows):
            block[cells(j), 0:MAIN] = stream[cells(j + 2), 0:MAIN] + main[i * CELLS : (i + 1) * CELLS]
            block[cells(j), MAIN:CH] = stream[cells(j + 2), MAIN:CH] + rest[i * CELLS : (i + 1) * CELLS]

    block_rows((1, 2, 3))
    for i in range(ROWS):
        row_stats(i, block[cells(i + 1), :])
    near3 = send_stats(1)

    stream[cells(0), :] = dot(cells_of(s), cin_w[2])
    stream[cells(8), :] = dot(cells_of(s + 2), cin_w[4])
    norm1(0)
    norm1(8)
    hidden_rows((0, 6))
    norm2(0)
    norm2(6)
    block_rows((0, 4))

    mean3, inv3 = take_stats(1, near3)

    same = ((iota((CELLS, CELLS), 0) ^ iota((CELLS, CELLS), 1)) & (COLS - 1)) == 0
    low_half = iota((CELLS, 128), 1) < HEAD_DIM

    def project(rows):
        projected[rows, :] = dot(((block[rows, :] - mean3) * inv3).astype(BF), wqkv[...]).astype(BF)

    def mix(rows):
        block[rows, :] += dot(attended[rows, :], wproj[...])

    own_cells = cells(1, ROWS)
    project(own_cells)

    def attend_row(i):
        row = cells(i)
        ones = jnp.ones((CELLS, 128), BF)

        def head(h):
            qt = projected[row, h // 2 * 128 : h // 2 * 128 + 128]
            if h < HEADS - 1:
                qt = jnp.where(low_half if h % 2 == 0 else jnp.logical_not(low_half), qt, jnp.zeros_like(qt))
            kt = projected[row, 384 + h // 2 * 128 : 512 + h // 2 * 128]
            vt = projected[row, 640 + (h + 1) // 2 * 128 : 768 + (h + 1) // 2 * 128]
            sc = jnp.where(same, dot_nt(qt, kt), -1e30)
            p = jnp.exp(sc - jnp.max(sc, axis=1, keepdims=True)).astype(BF)
            o = dot(p, jnp.concatenate([vt, ones], axis=1))
            return o[:, 0:128] / o[:, 128:256]

        attended[row, 0:128] = jnp.where(low_half, 0.0, head(0)).astype(BF)
        attended[row, 128:256] = jnp.where(low_half, head(1), head(2)).astype(BF)
        attended[row, 256:384] = jnp.where(low_half, head(3), head(4)).astype(BF)

    for i in range(1, ROWS + 1):
        attend_row(i)
    mix(own_cells)
    for i in range(ROWS):
        row_stats(i, block[cells(i + 1), :])
    near4 = send_stats(2)

    for i in (0, ROWS + 1):
        project(cells(i))

    for i in (0, ROWS + 1):
        attend_row(i)
    for i in (0, ROWS + 1):
        mix(cells(i))

    load_cout.wait()
    cout_f[36:40, :] = jnp.zeros((4, CH), F32)
    for a in range(3):
        for b in range(3):
            r = (a * 3 + b) * 4
            cout_f[r : r + 4, :] = cout_v[a, b].astype(F32)
    to = iota((48, 40), 0)
    src = iota((48, 40), 1)
    to_b = to >> 4
    to_row = to & 15
    to_c = to_row * 21846 >> 16
    for i in range(ROWS + 2):
        tap = i - (to_row - 3 * to_c)
        hit = (tap >= 0) & (tap < 3) & (to_row < 12) & (src == (tap * 3 + to_b) * 4 + to_c)
        wout[i] = dot(jnp.where(hit, 1.0, 0.0).astype(BF), cout_f[...].astype(BF)).astype(BF)

    step_of = iota((8, 128), 0) * 128 + iota((8, 128), 1)
    lo, hi = 0.00085**0.5, 0.012**0.5
    beta = (lo + step_of.astype(F32) * ((hi - lo) / 999.0)) ** 2

    def alpha(t):
        v = jnp.where(step_of <= t, 1.0 - beta, 1.0)
        for sh in (64, 32, 16, 8, 4, 2, 1):
            v = v * pltpu.roll(v, sh, 1)
        for sh in (4, 2, 1):
            v = v * pltpu.roll(v, sh, 0)
        return v[0:1, 0:1]

    alpha_now = alpha(level)
    alpha_next = alpha(level - STEP)
    keep = jnp.sqrt(alpha_next / alpha_now)
    gain = jnp.sqrt(1.0 - alpha_next) - keep * jnp.sqrt(1.0 - alpha_now)

    mean4, inv4 = take_stats(2, near4)
    half_inv4 = 0.5 * inv4

    z = jnp.zeros((48, CELLS), F32)
    for i in range(ROWS + 2):
        row = s * ROWS + i - 1
        inside = jnp.where((row >= 0) & (row < ns * ROWS), half_inv4, 0.0)
        z = z + dot_nt(wout[i], silu_of_half((block[cells(i), :] - mean4) * inside).astype(BF))
    lane = iota((16, CELLS), 1) & (COLS - 1)
    noise = (
        z[16:32]
        + jnp.where(lane == 0, 0.0, pltpu.roll(z[0:16], 1, 1))
        + jnp.where(lane == COLS - 1, 0.0, pltpu.roll(z[32:48], CELLS - 1, 1))
    )
    main_out[...] = keep * lat_f[...] + gain * noise
    main_send_copy = pltpu.make_async_remote_copy(
        main_out, main_in, main_send, main_recv, device_id=(ahead, s), device_id_type=MESH
    )
    main_send_copy.start()

    def put(out, v):
        for f in range(FRAMES):
            out[pl.ds(f, 12, stride=FRAMES), :] = v[0:12, f * COLS : (f + 1) * COLS]

    put(noise_ref, noise)
    main_send_copy.wait_recv()
    put(next_ref, main_in[...])

    pltpu.make_async_copy(lat_b.at[pl.ds(0, (ns - 1) * 16)], lat_b.at[pl.ds(0, (ns - 1) * 16)], lat_send).wait()
    for phase in range(3):
        stats_sent(phase)
    main_send_copy.wait_send()


def per_device(
    nq,
    ns,
    latents,
    fresh_noise,
    timesteps,
    queue_map,
    conv_in_w,
    time_w1,
    time_w2,
    emb_w,
    conv1_w,
    conv2_w,
    qkv_w,
    proj_w,
    conv_out_w,
):
    hbm = pl.BlockSpec(memory_space=pltpu.HBM)
    vmem = pl.BlockSpec(memory_space=pltpu.VMEM)
    latents = jnp.transpose(latents[0], (0, 2, 1, 3)).reshape(4 * ROWS * FRAMES, COLS)
    emb_t = emb_w.T
    out_t = jnp.swapaxes(conv_out_w, 2, 3)
    weights = (conv_in_w, time_w1, time_w2, emb_t, conv1_w, conv2_w, qkv_w, proj_w, out_t)
    DMA = pltpu.SemaphoreType.DMA
    operands = [
        pltpu.with_memory_space_constraint(v, pltpu.HBM) for v in (timesteps, queue_map, latents, *weights)
    ]
    noise, nxt = pl.pallas_call(
        functools.partial(kernel, nq, ns),
        out_shape=(
            jax.ShapeDtypeStruct((4 * ROWS * FRAMES, COLS), F32),
            jax.ShapeDtypeStruct((4 * ROWS * FRAMES, COLS), F32),
        ),
        in_specs=[hbm] * len(operands),
        out_specs=(vmem, vmem),
        scratch_shapes=[pltpu.SMEM(timesteps.shape, jnp.int32), pltpu.SMEM(queue_map.shape, jnp.int32)]
        + [pltpu.VMEM(latents.shape, F32)]
        + [pltpu.VMEM(w.shape, BF) for w in weights]
        + [
            DMA((len(operands),)),
            pltpu.VMEM((16, CELLS), F32),
            pltpu.VMEM(((ns + 4) * 16, CELLS), BF),
            pltpu.VMEM((3, (ns + 4) * 16, CELLS), BF),
            pltpu.VMEM((40, CH), F32),
            pltpu.VMEM((7, 144, CH), BF),
            pltpu.VMEM((9 * CELLS, CH), F32),
            pltpu.VMEM((7 * CELLS, CH), F32),
            pltpu.VMEM((5 * CELLS, CH), F32),
            pltpu.VMEM((9 * CELLS, MAIN), BF),
            pltpu.VMEM((11 * CELLS, 256), BF),
            pltpu.VMEM((7 * CELLS, MAIN), BF),
            pltpu.VMEM((9 * CELLS, 256), BF),
            pltpu.VMEM((2, 3, 256, MAIN), BF),
            pltpu.VMEM((2, 1024, 256), BF),
            pltpu.VMEM((CH, 1024), BF),
            pltpu.VMEM((384, CH), BF),
            pltpu.VMEM(((ROWS + 2) * CELLS, 1024), BF),
            pltpu.VMEM((CH, CH), BF),
            pltpu.VMEM((1, CH), F32),
            pltpu.VMEM((40, CH), F32),
            pltpu.VMEM((5, 48, CH), BF),
            pltpu.VMEM(((ROWS + 2) * CELLS, 384), BF),
            pltpu.VMEM((2, 8, CH), F32),
            pltpu.VMEM((3, ns, 2, CH), F32),
            pltpu.VMEM((16, CELLS), F32),
            pltpu.VMEM((16, CELLS), F32),
            DMA,
            DMA((5,)),
            DMA((3,)),
            DMA((3,)),
            DMA,
            DMA,
        ],
        compiler_params=pltpu.CompilerParams(
            collective_id=0, has_side_effects=True, vmem_limit_bytes=44 * 1024 * 1024
        ),
        cost_estimate=pl.CostEstimate(flops=10**10, bytes_accessed=10**7, transcendentals=10**6),
    )(*operands)

    def as_frames(v):
        return jnp.transpose(v.reshape(4, ROWS, FRAMES, COLS), (0, 2, 1, 3))

    next_queue = jnp.where(lax.axis_index("queue") == 0, fresh_noise, as_frames(nxt))
    return as_frames(noise)[None], next_queue[None]


def solution(mesh):
    nq, ns = mesh.shape["queue"], mesh.shape["space"]
    rows = P("queue", None, None, "space", None)
    return jax.shard_map(
        functools.partial(per_device, nq, ns),
        mesh=mesh,
        in_specs=(rows, P(None, None, "space", None)) + (P(),) * 11,
        out_specs=(rows, rows),
        check_vma=False,
    )
```
